512 devices in a mesh: rows: 64 (over z, x, core), rep: 8 (over y).
Axes of the slice: x: 4, y: 8, z: 8, core: 2. Of those that a mesh axis runs over, the one named last changes fastest.
Arguments:
- features: bfloat16 [65536, 128], P(('rows', 'rep')), may hold values from -6 to 6
- degrees: int32 [65536], P(('rows', 'rep')), may hold values from 0 to 16
- tile_values: bfloat16 [49152, 128, 128], P(('rows', 'rep')), may hold values from 0 to 0.099609375
- tile_row: int32 [49152], P(('rows', 'rep')), may hold values from 0 to 511, as said below
- tile_col: int32 [49152], P(('rows', 'rep')), may hold values from 0 to 511, as said below
- tile_count: int32 [512], P(('rows', 'rep')), may hold values from 24 to 96, as said below
- weight: bfloat16 [128, 64], replicated, may hold values from -0.5 to 0.5
- out_bias: bfloat16 [64], replicated, may hold values from -3 to 3
- cotangent: bfloat16 [65536, 64], P(('rows', 'rep')), may hold values from -6 to 6
Outputs:
- mixed: bfloat16 [65536, 64], P(('rows', 'rep'))
- grad_features: bfloat16 [65536, 128], P(('rows', 'rep'))
- grad_weight: float32 [128, 64], replicated
The draws below stay inside these ranges and needn't reach their ends.
Inputs may be any that keep to these rules, and one draw needn't show every extreme that they name: `tile_row`: on the device with rows index r and rep index p, every slot's row block lies in r * 8 to r * 8 + 7; the (row block, column block) pairs of one device's slots are all different. `tile_col`: on the device with rep index p, every slot's column block c has c % 8 == p. `tile_count`: some device has all 96 slots live.
All inputs are finite; a program needn't handle non-finite values.
Results may differ from the reference program's by a relative error of at most 0.015.
Values may be sent and summed in bfloat16 or wider, within the bound.
No kernel may reach another device: no remote copies, remote signals or barrier semaphores. Data moves between devices by JAX's collectives and lax.ppermute only.
A program may use at most 64 MiB of HBM per device.

```python
import jax
import jax.numpy as jnp
from jax import lax

BLOCK = 128
F_IN = 128
F_OUT = 64
TPD = 96
NODES = 65536
TILES = 49152
N_ROWS = 64
N_REP = 8
DEVICES = 512


def tile_pattern(key):
    device_keys = jax.random.split(key, DEVICES)
    orders = jax.vmap(lambda one_key: jax.random.permutation(one_key, N_REP * N_ROWS))(device_keys)[:, :TPD]
    device_ids = jnp.arange(DEVICES, dtype=jnp.int32)
    row_ids = device_ids // N_REP
    rep_ids = device_ids % N_REP
    tile_rows = row_ids[:, None] * N_REP + orders // N_ROWS
    tile_cols = orders % N_ROWS * N_REP + rep_ids[:, None]
    shrink = jax.random.randint(jax.random.fold_in(key, 11), (DEVICES,), 1, 5)
    counts = TPD // shrink
    chosen = jax.random.randint(jax.random.fold_in(key, 12), (), 0, DEVICES)
    counts = jnp.where(device_ids == chosen, TPD, counts)
    return (tile_rows.reshape(-1).astype(jnp.int32), tile_cols.reshape(-1).astype(jnp.int32), counts.astype(jnp.int32))


def draw_tile_row(key, part):
    return tile_pattern(key)[0]


def draw_tile_col(key, part):
    return tile_pattern(key)[1]


def draw_tile_count(key, part):
    return tile_pattern(key)[2]


def touch_ends(drawn, key, smallest, top_value):
    longest = drawn.shape.index(max(drawn.shape))
    spots = []
    for shift in (0, 1):
        where = [jax.random.randint(jax.random.fold_in(key, axis), (), 0, length) for axis, length in enumerate(drawn.shape)]
        where[longest] = (where[longest] + shift) % drawn.shape[longest]
        spots.append(tuple(where))
    return drawn.at[spots[0]].set(smallest).at[spots[1]].set(top_value)


def levels(key, dims, pieces, least, largest):
    gain = 1.0
    for dim, shards_of in pieces:
        draws = jax.random.uniform(jax.random.fold_in(jax.random.fold_in(key, 6), dim), (shards_of,), jnp.float32, least / len(pieces), largest / len(pieces))
        gain = gain * jnp.repeat(jnp.exp(draws), dims[dim] // shards_of).reshape((-1,) + (1,) * (len(dims) - 1 - dim))
    return gain


def gaussian(rng, shape, width, limit, cuts=(), kind=jnp.bfloat16):
    result = jax.random.normal(rng, shape, jnp.float32) * width
    if len(cuts) > 0:
        result = levels(rng, shape, cuts, -0.22, 0.18) * result
    return jnp.clip(result, min=-limit, max=limit).astype(kind)


def setup_inputs(seed: int = 0) -> dict:
    arg_keys = jax.random.split(jax.random.key(seed), 10)
    features = gaussian(arg_keys[0], (NODES, F_IN), 1.0, 6.0, ((0, 512),))
    degrees = touch_ends(jax.random.randint(arg_keys[1], (NODES,), 0, 17), jax.random.fold_in(arg_keys[1], 1), 0, 16).astype(jnp.int32)
    tile_values = jnp.clip(0.099609375 * jax.random.uniform(arg_keys[2], (TILES, BLOCK, BLOCK), jnp.float32) ** levels(arg_keys[2], (TILES, BLOCK, BLOCK), ((0, 512),), -0.2, 0.2), 0.0, 0.099609375).astype(jnp.bfloat16)
    tile_row = draw_tile_row(jax.random.fold_in(arg_keys[9], 71), 0)
    tile_col = draw_tile_col(jax.random.fold_in(arg_keys[9], 71), 0)
    tile_count = draw_tile_count(jax.random.fold_in(arg_keys[9], 71), 0)
    weight = gaussian(arg_keys[6], (F_IN, F_OUT), F_IN ** -0.5, 0.5)
    out_bias = gaussian(arg_keys[7], (F_OUT,), 0.5, 3.0)
    cotangent = gaussian(arg_keys[8], (NODES, F_OUT), 1.0, 6.0, ((0, 512),))
    return dict(features=features, degrees=degrees, tile_values=tile_values, tile_row=tile_row, tile_col=tile_col, tile_count=tile_count, weight=weight, out_bias=out_bias, cotangent=cotangent)


def silu_slope(preact):
    sigmoid_val = jax.nn.sigmoid(preact)
    return sigmoid_val * (1.0 + preact * (1.0 - sigmoid_val))

def reference(features, degrees, tile_values, tile_row, tile_col, tile_count, weight, out_bias, cotangent):
    scales = lax.rsqrt(degrees.astype(jnp.float32) + 1.0)
    scaled = (scales[:, None] * features.astype(jnp.float32)).astype(jnp.bfloat16)
    nblocks = NODES // BLOCK
    scaled_blocks = scaled.astype(jnp.float32).reshape(nblocks, BLOCK, F_IN)
    value_sets = tile_values.reshape(DEVICES, TPD, BLOCK, BLOCK)
    row_sets = tile_row.reshape(DEVICES, TPD)
    col_sets = tile_col.reshape(DEVICES, TPD)
    live_sets = (jnp.arange(TPD)[None, :] < tile_count[:, None]).astype(jnp.float32)

    def forward_device(running, member):
        values, rows_here, cols_here, live_here = member
        product = jnp.einsum('tij,tjf->tif', values.astype(jnp.float32), scaled_blocks[cols_here])
        return (running.at[rows_here].add(product * live_here[:, None, None]), None)
    propagated, _ = lax.scan(forward_device, jnp.zeros((nblocks, BLOCK, F_IN), jnp.float32), (value_sets, row_sets, col_sets, live_sets))
    aggregated = (scales[:, None] * (propagated.reshape(NODES, F_IN) + scaled.astype(jnp.float32))).astype(jnp.bfloat16)
    preact = jnp.dot(aggregated, weight, preferred_element_type=jnp.float32) + out_bias.astype(jnp.float32)
    mixed = jax.nn.silu(preact).astype(jnp.bfloat16)
    grad_pre = (cotangent.astype(jnp.float32) * silu_slope(preact)).astype(jnp.bfloat16)
    grad_weight = jnp.einsum('nf,ng->fg', aggregated.astype(jnp.float32), grad_pre.astype(jnp.float32)) / jnp.sqrt(jnp.float32(NODES))
    lifted = (scales[:, None] * grad_pre.astype(jnp.float32)).astype(jnp.bfloat16)
    lifted_blocks = lifted.astype(jnp.float32).reshape(nblocks, BLOCK, F_OUT)

    def backward_device(running, member):
        values, rows_here, cols_here, live_here = member
        product = jnp.einsum('tij,tif->tjf', values.astype(jnp.float32), lifted_blocks[rows_here])
        return (running.at[cols_here].add(product * live_here[:, None, None]), None)
    pulled, _ = lax.scan(backward_device, jnp.zeros((nblocks, BLOCK, F_OUT), jnp.float32), (value_sets, row_sets, col_sets, live_sets))
    grad_scaled = (scales[:, None] * (pulled.reshape(NODES, F_OUT) + lifted.astype(jnp.float32))).astype(jnp.bfloat16)
    grad_features = jnp.dot(grad_scaled, weight.T, preferred_element_type=jnp.float32).astype(jnp.bfloat16)
    return (mixed, grad_features, grad_weight)
```

```python
import numpy as np

import jax
import jax.numpy as jnp
from jax import lax
from jax.experimental import pallas as pl
from jax.experimental.pallas import tpu as pltpu
from jax.sharding import Mesh, PartitionSpec as P

N_Z, N_X, N_C, N_Y = 8, 4, 2, 8
BLOCK = 128
F_IN = 128
F_OUT = 64
CHUNK = 8
HALF = N_X * N_Z
VMEM_BYTES = 32 * 1024 * 1024
f32 = jnp.float32
bf16 = jnp.bfloat16


def scale_row(degrees_ref):
    return lax.rsqrt(degrees_ref[...].astype(f32) + 1.0)


def scale_square(degrees_ref):
    return jnp.transpose(jnp.broadcast_to(scale_row(degrees_ref), (BLOCK, BLOCK)))


def place_of(col, core):
    owner = lax.shift_right_logical(col, 3)
    z = lax.shift_right_logical(owner, 3)
    x = jnp.bitwise_and(lax.shift_right_logical(owner, 1), 3)
    other = jnp.bitwise_xor(jnp.bitwise_and(owner, 1), core)
    return other * HALF + x * N_Z + z


def start_kernel(degrees_ref, features_ref, scaled_ref):
    scaled = (scale_square(degrees_ref) * features_ref[...].astype(f32)).astype(bf16)
    scaled_ref[...] = jnp.broadcast_to(scaled[None], scaled_ref.shape)


def chunk_copy(values_ref, held, sems, i):
    return pltpu.make_async_copy(
        values_ref.at[pl.ds(i * CHUNK, CHUNK)], held.at[pl.ds(i * CHUNK, CHUNK)], sems.at[i]
    )


def forward_kernel(
    rows_ref, cols_ref, count_ref, core_ref, own_ref, other_ref, values_ref, out_ref, held, gathered, acc, sems, gsems
):
    count = count_ref[0]
    core = core_ref[0]
    chunks = lax.div(count + (CHUNK - 1), CHUNK)
    own_copy = pltpu.make_async_copy(own_ref, gathered.at[pl.ds(0, HALF)], gsems.at[0])
    other_copy = pltpu.make_async_copy(other_ref, gathered.at[pl.ds(HALF, HALF)], gsems.at[1])
    own_copy.start()
    other_copy.start()

    def start(i, carry):
        chunk_copy(values_ref, held, sems, i).start()
        return carry

    lax.fori_loop(0, chunks, start, 0)
    acc[...] = jnp.zeros_like(acc)
    own_copy.wait()
    other_copy.wait()

    def chunk(i, carry):
        chunk_copy(values_ref, held, sems, i).wait()
        for g in range(0, CHUNK, 4):
            products = []
            for k in range(g, g + 4):
                t = i * CHUNK + k
                place = place_of(cols_ref[t], core)
                products.append(jnp.dot(held[t], gathered[place], preferred_element_type=f32))
            for k in range(g, g + 4):
                t = i * CHUNK + k
                row = jnp.where(t < count, jnp.bitwise_and(rows_ref[t], N_Y - 1), N_Y)
                acc[row] += products[k - g]
        return carry

    lax.fori_loop(0, chunks, chunk, 0)
    out_ref[...] = acc[0:N_Y].astype(bf16)


def middle_kernel(
    degrees_ref, parts_ref, scaled_ref, weight_ref, bias_ref, cotangent_ref, mixed_ref, send_ref
):
    total = jnp.sum(parts_ref[...].astype(f32), axis=0) + scaled_ref[0].astype(f32)
    aggregated = (scale_square(degrees_ref) * total).astype(bf16)
    preact = (
        lax.dot_general(weight_ref[...], aggregated, (((1,), (1,)), ((), ())), preferred_element_type=f32)
        + bias_ref[...]
    )
    gate = jax.nn.sigmoid(preact)
    mixed_ref[...] = (preact * gate).astype(bf16)
    slope = gate * (1.0 + preact * (1.0 - gate))
    grad_pre = (cotangent_ref[...].astype(f32) * slope).astype(bf16)
    lifted = (scale_row(degrees_ref) * grad_pre.astype(f32)).astype(bf16)
    weight_part = jnp.dot(grad_pre, aggregated, preferred_element_type=f32).astype(bf16)
    send_ref[:, 0] = jnp.broadcast_to(lifted[None], (N_Y, F_OUT, BLOCK))
    send_ref[:, 1] = jnp.broadcast_to(weight_part[None], (N_Y, F_OUT, F_IN))


def backward_kernel(
    rows_ref, cols_ref, count_ref, core_ref, group_ref, values_ref, keep_ref, send_ref, held, acc, sems
):
    count = count_ref[0]
    core = core_ref[0]
    chunks = lax.div(count + (CHUNK - 1), CHUNK)

    def start(i, carry):
        chunk_copy(values_ref, held, sems, i).start()
        return carry

    lax.fori_loop(0, chunks, start, 0)
    acc[...] = jnp.zeros_like(acc)

    def chunk(i, carry):
        chunk_copy(values_ref, held, sems, i).wait()
        for g in range(0, CHUNK, 4):
            products = []
            for k in range(g, g + 4):
                t = i * CHUNK + k
                row = jnp.bitwise_and(rows_ref[t], N_Y - 1)
                products.append(jnp.dot(group_ref[row, 0], held[t], preferred_element_type=f32))
            for k in range(g, g + 4):
                t = i * CHUNK + k
                place = jnp.where(t < count, place_of(cols_ref[t], core), 2 * HALF)
                acc[place] += products[k - g]
        return carry

    lax.fori_loop(0, chunks, chunk, 0)
    weight_part = jnp.sum(group_ref[:, 1].astype(f32), axis=0).astype(bf16)
    for x in range(N_X):
        keep_ref[x, 0:N_Z] = acc[x * N_Z : (x + 1) * N_Z].astype(bf16)
        send_ref[x, 0:N_Z] = acc[HALF + x * N_Z : HALF + (x + 1) * N_Z].astype(bf16)
        keep_ref[x, N_Z] = weight_part
        send_ref[x, N_Z] = weight_part


def core_sum_kernel(keep_ref, recv_ref, out_ref):
    out_ref[...] = (keep_ref[...].astype(f32) + recv_ref[...].astype(f32)).astype(bf16)


def x_sum_kernel(recv_ref, out_ref):
    total = jnp.sum(recv_ref[...].astype(f32), axis=0).astype(bf16)
    out_ref[:, 0] = total[0:N_Z]
    out_ref[:, 1] = jnp.broadcast_to(total[N_Z][None], (N_Z, F_OUT, F_IN))


def final_kernel(degrees_ref, recv_ref, sent_ref, weight_ref, grad_features_ref, grad_weight_ref):
    total = jnp.sum(recv_ref[...].astype(f32), axis=0)
    grad_scaled = scale_row(degrees_ref) * (total[0] + sent_ref[0, 0].astype(f32))
    turned = jnp.transpose(grad_scaled).astype(bf16)
    grad_features_ref[...] = jnp.dot(turned, weight_ref[...], preferred_element_type=f32).astype(bf16)
    node_total = BLOCK * N_Z * N_X * N_C * N_Y
    grad_weight_ref[...] = total[1] * (1.0 / np.sqrt(node_total))


def vmem():
    return pl.BlockSpec(memory_space=pltpu.VMEM)


def smem():
    return pl.BlockSpec(memory_space=pltpu.SMEM)


def shards(
    features, degrees, tile_values, tile_row, tile_col, tile_count, weight, out_bias, cotangent
):
    slots = tile_values.shape[0]
    core = lax.axis_index("c").astype(jnp.int32).reshape(1)
    degrees = degrees.reshape(1, BLOCK)
    weight_t = weight.T
    cotangent_t = cotangent.T
    bias = jnp.broadcast_to(out_bias.astype(f32)[:, None], (F_OUT, BLOCK))
    params = pltpu.CompilerParams(vmem_limit_bytes=VMEM_BYTES)

    scaled = pl.pallas_call(
        start_kernel,
        out_shape=jax.ShapeDtypeStruct((N_Z, BLOCK, F_IN), bf16),
        in_specs=[vmem(), vmem()],
        out_specs=vmem(),
        compiler_params=params,
        name="start",
    )(degrees, features)
    by_z = lax.all_to_all(scaled, "z", 0, 0)
    by_xz = lax.all_to_all(jnp.broadcast_to(by_z[None], (N_X,) + by_z.shape), "x", 0, 0)
    own = by_xz.reshape(HALF, BLOCK, F_IN)
    other = lax.ppermute(own, "c", [(0, 1), (1, 0)])

    parts = pl.pallas_call(
        forward_kernel,
        out_shape=jax.ShapeDtypeStruct((N_Y, BLOCK, F_IN), bf16),
        in_specs=[smem()] * 4 + [pl.BlockSpec(memory_space=pl.ANY)] * 3,
        out_specs=vmem(),
        scratch_shapes=[
            pltpu.VMEM((slots, BLOCK, BLOCK), bf16),
            pltpu.VMEM((2 * HALF, BLOCK, F_IN), bf16),
            pltpu.VMEM((N_Y + 1, BLOCK, F_IN), f32),
            pltpu.SemaphoreType.DMA((slots // CHUNK,)),
            pltpu.SemaphoreType.DMA((2,)),
        ],
        compiler_params=params,
        name="forward",
    )(tile_row, tile_col, tile_count, core, own, other, tile_values)
    parts = lax.all_to_all(parts, "y", 0, 0)

    mixed_t, send = pl.pallas_call(
        middle_kernel,
        out_shape=(
            jax.ShapeDtypeStruct((F_OUT, BLOCK), bf16),
            jax.ShapeDtypeStruct((N_Y, 2, F_OUT, BLOCK), bf16),
        ),
        in_specs=[vmem()] * 6,
        out_specs=(vmem(), vmem()),
        compiler_params=params,
        name="middle",
    )(degrees, parts, scaled, weight_t, bias, cotangent_t)
    group = lax.all_to_all(send, "y", 0, 0)

    half = jax.ShapeDtypeStruct((N_X, N_Z + 1, F_OUT, BLOCK), bf16)
    keep, away = pl.pallas_call(
        backward_kernel,
        out_shape=(half, half),
        in_specs=[smem()] * 4 + [vmem(), pl.BlockSpec(memory_space=pl.ANY)],
        out_specs=(vmem(), vmem()),
        scratch_shapes=[
            pltpu.VMEM((slots, BLOCK, BLOCK), bf16),
            pltpu.VMEM((2 * HALF + 1, F_OUT, BLOCK), f32),
            pltpu.SemaphoreType.DMA((slots // CHUNK,)),
        ],
        compiler_params=params,
        name="backward",
    )(tile_row, tile_col, tile_count, core, group, tile_values)
    recv = lax.ppermute(away, "c", [(0, 1), (1, 0)])
    by_core = pl.pallas_call(
        core_sum_kernel,
        out_shape=half,
        in_specs=[vmem()] * 2,
        out_specs=vmem(),
        compiler_params=params,
        name="core_sum",
    )(keep, recv)
    by_x = lax.all_to_all(by_core, "x", 0, 0)
    by_x = pl.pallas_call(
        x_sum_kernel,
        out_shape=jax.ShapeDtypeStruct((N_Z, 2, F_OUT, BLOCK), bf16),
        in_specs=[vmem()],
        out_specs=vmem(),
        compiler_params=params,
        name="x_sum",
    )(by_x)
    last = lax.all_to_all(by_x, "z", 0, 0)
    grad_features, grad_weight_t = pl.pallas_call(
        final_kernel,
        out_shape=(
            jax.ShapeDtypeStruct((BLOCK, F_IN), bf16),
            jax.ShapeDtypeStruct((F_OUT, F_IN), f32),
        ),
        in_specs=[vmem()] * 4,
        out_specs=(vmem(), vmem()),
        compiler_params=params,
        name="final",
    )(degrees, last, send, weight_t)
    return (mixed_t.T, grad_features, grad_weight_t.T)


def solution(mesh):
    devices = np.asarray(mesh.devices).reshape(N_Z, N_X, N_C, N_Y)
    fine = Mesh(devices, ("z", "x", "c", "y"))
    every = ("z", "x", "c", "y")
    in_specs = (
        P(every, None),
        P(every),
        P(every, None, None),
        P(every),
        P(every),
        P(every),
        P(),
        P(),
        P(every, None),
    )
    out_specs = (P(every, None), P(every, None), P())
    return jax.shard_map(shards, mesh=fine, in_specs=in_specs, out_specs=out_specs, check_vma=False)
```

```python
import numpy as np

import jax
import jax.numpy as jnp
from jax import lax
from jax.experimental import pallas as pl
from jax.experimental.pallas import tpu as pltpu
from jax.sharding import Mesh, PartitionSpec as P

N_Z, N_X, N_C, N_Y = 8, 4, 2, 8
BLOCK = 128
F_IN = 128
F_OUT = 64
CHUNK = 48
GROUP = 8
HALF = N_X * N_Z
VMEM_BYTES = 16 * 1024 * 1024
f32 = jnp.float32
bf16 = jnp.bfloat16


def scale_row(degrees_ref):
    return lax.rsqrt(degrees_ref[...].astype(f32) + 1.0)


def scale_square(degrees_ref):
    return jnp.transpose(jnp.broadcast_to(scale_row(degrees_ref), (BLOCK, BLOCK)))


def place_of(col, core):
    owner = lax.shift_right_logical(col, 3)
    z = lax.shift_right_logical(owner, 3)
    x = jnp.bitwise_and(lax.shift_right_logical(owner, 1), 3)
    other = jnp.bitwise_xor(jnp.bitwise_and(owner, 1), core)
    return other * HALF + x * N_Z + z


def start_kernel(degrees_ref, features_ref, scaled_ref, degrees_here, features_here, sems):
    degrees_copy = pltpu.make_async_copy(degrees_ref, degrees_here, sems.at[0])
    features_copy = pltpu.make_async_copy(features_ref, features_here, sems.at[1])
    degrees_copy.start()
    features_copy.start()
    degrees_copy.wait()
    square = scale_square(degrees_here)
    features_copy.wait()
    scaled = (square * features_here[...].astype(f32)).astype(bf16)
    scaled_ref[...] = jnp.broadcast_to(scaled[None], scaled_ref.shape)


def forward_kernel(
    rows_ref, cols_ref, count_ref, core_ref, own_ref, other_ref, values_ref, out_ref, gathered, acc
):
    count = count_ref[0]
    core = core_ref[0]
    gathered[0:HALF] = own_ref[...]
    gathered[HALF : 2 * HALF] = other_ref[...]
    acc[...] = jnp.zeros_like(acc)

    def chunk(i, carry):
        for g in range(0, CHUNK, GROUP):
            slots = [i * CHUNK + g + k for k in range(GROUP)]
            products = [
                jnp.dot(values_ref[t], gathered[place_of(cols_ref[t], core)], preferred_element_type=f32)
                for t in slots
            ]
            for t, product in zip(slots, products):
                row = jnp.where(t < count, jnp.bitwise_and(rows_ref[t], N_Y - 1), N_Y)
                acc[row] += product
        return carry

    lax.fori_loop(0, values_ref.shape[0] // CHUNK, chunk, 0)
    out_ref[...] = acc[0:N_Y].astype(bf16)


def middle_kernel(
    degrees_ref, parts_ref, scaled_ref, weight_ref, bias_ref, cotangent_ref, mixed_ref, send_ref
):
    total = jnp.sum(parts_ref[...].astype(f32), axis=0) + scaled_ref[0].astype(f32)
    aggregated = (scale_square(degrees_ref) * total).astype(bf16)
    preact = (
        lax.dot_general(weight_ref[...], aggregated, (((1,), (1,)), ((), ())), preferred_element_type=f32)
        + bias_ref[...]
    )
    gate = jax.nn.sigmoid(preact)
    mixed_ref[...] = (preact * gate).astype(bf16)
    slope = gate * (1.0 + preact * (1.0 - gate))
    grad_pre = (cotangent_ref[...].astype(f32) * slope).astype(bf16)
    lifted = (scale_row(degrees_ref) * grad_pre.astype(f32)).astype(bf16)
    weight_part = jnp.dot(grad_pre, aggregated, preferred_element_type=f32).astype(bf16)
    send_ref[:, 0] = jnp.broadcast_to(lifted[None], (N_Y, F_OUT, BLOCK))
    send_ref[:, 1] = jnp.broadcast_to(weight_part[None], (N_Y, F_OUT, F_IN))


def backward_kernel(
    rows_ref, cols_ref, count_ref, core_ref, group_ref, values_ref, keep_ref, send_ref, acc
):
    count = count_ref[0]
    core = core_ref[0]
    acc[...] = jnp.zeros_like(acc)

    def chunk(i, carry):
        for g in range(0, CHUNK, GROUP):
            slots = [i * CHUNK + g + k for k in range(GROUP)]
            products = [
                jnp.dot(
                    group_ref[jnp.bitwise_and(rows_ref[t], N_Y - 1), 0],
                    values_ref[t],
                    preferred_element_type=f32,
                )
                for t in slots
            ]
            for t, product in zip(slots, products):
                place = jnp.where(t < count, place_of(cols_ref[t], core), 2 * HALF)
                acc[place] += product
        return carry

    lax.fori_loop(0, values_ref.shape[0] // CHUNK, chunk, 0)
    weight_part = jnp.sum(group_ref[:, 1].astype(f32), axis=0).astype(bf16)
    for x in range(N_X):
        keep_ref[x, 0:N_Z] = acc[x * N_Z : (x + 1) * N_Z].astype(bf16)
        send_ref[x, 0:N_Z] = acc[HALF + x * N_Z : HALF + (x + 1) * N_Z].astype(bf16)
        keep_ref[x, N_Z] = weight_part
        send_ref[x, N_Z] = weight_part


def core_sum_kernel(keep_ref, recv_ref, out_ref):
    out_ref[...] = (keep_ref[...].astype(f32) + recv_ref[...].astype(f32)).astype(bf16)


def x_sum_kernel(recv_ref, out_ref):
    total = jnp.sum(recv_ref[...].astype(f32), axis=0).astype(bf16)
    out_ref[:, 0] = total[0:N_Z]
    out_ref[:, 1] = jnp.broadcast_to(total[N_Z][None], (N_Z, F_OUT, F_IN))


def final_kernel(degrees_ref, recv_ref, sent_ref, weight_ref, grad_features_ref, grad_weight_ref):
    total = jnp.sum(recv_ref[...].astype(f32), axis=0)
    grad_scaled = scale_row(degrees_ref) * (total[0] + sent_ref[0, 0].astype(f32))
    turned = jnp.transpose(grad_scaled).astype(bf16)
    grad_features_ref[...] = jnp.dot(turned, weight_ref[...], preferred_element_type=f32).astype(bf16)
    node_total = BLOCK * N_Z * N_X * N_C * N_Y
    grad_weight_ref[...] = total[1] * (1.0 / np.sqrt(node_total))


def vmem():
    return pl.BlockSpec(memory_space=pltpu.VMEM)


def smem():
    return pl.BlockSpec(memory_space=pltpu.SMEM)


def shards(
    features, degrees, tile_values, tile_row, tile_col, tile_count, weight, out_bias, cotangent
):
    core = lax.axis_index("c").astype(jnp.int32).reshape(1)
    degrees = degrees.reshape(1, BLOCK)
    weight_t = weight.T
    cotangent_t = cotangent.T
    bias = jnp.broadcast_to(out_bias.astype(f32)[:, None], (F_OUT, BLOCK))
    params = pltpu.CompilerParams(vmem_limit_bytes=VMEM_BYTES)

    scaled = pl.pallas_call(
        start_kernel,
        out_shape=jax.ShapeDtypeStruct((N_Z, BLOCK, F_IN), bf16),
        in_specs=[pl.BlockSpec(memory_space=pltpu.HBM)] * 2,
        out_specs=vmem(),
        scratch_shapes=[
            pltpu.VMEM((1, BLOCK), jnp.int32),
            pltpu.VMEM((BLOCK, F_IN), bf16),
            pltpu.SemaphoreType.DMA((2,)),
        ],
        compiler_params=params,
        name="start",
    )(degrees, features)
    by_z = lax.all_to_all(scaled, "z", 0, 0)
    by_xz = lax.all_to_all(jnp.broadcast_to(by_z[None], (N_X,) + by_z.shape), "x", 0, 0)
    own = by_xz.reshape(HALF, BLOCK, F_IN)
    other = lax.ppermute(own, "c", [(0, 1), (1, 0)])

    parts = pl.pallas_call(
        forward_kernel,
        out_shape=jax.ShapeDtypeStruct((N_Y, BLOCK, F_IN), bf16),
        in_specs=[smem()] * 4 + [vmem()] * 3,
        out_specs=vmem(),
        scratch_shapes=[
            pltpu.VMEM((2 * HALF, BLOCK, F_IN), bf16),
            pltpu.VMEM((N_Y + 1, BLOCK, F_IN), f32),
        ],
        compiler_params=params,
        name="forward",
    )(tile_row, tile_col, tile_count, core, own, other, tile_values)
    parts = lax.all_to_all(parts, "y", 0, 0)

    mixed_t, send = pl.pallas_call(
        middle_kernel,
        out_shape=(
            jax.ShapeDtypeStruct((F_OUT, BLOCK), bf16),
            jax.ShapeDtypeStruct((N_Y, 2, F_OUT, BLOCK), bf16),
        ),
        in_specs=[vmem()] * 6,
        out_specs=(vmem(), vmem()),
        compiler_params=params,
        name="middle",
    )(degrees, parts, scaled, weight_t, bias, cotangent_t)
    group = lax.all_to_all(send, "y", 0, 0)

    half = jax.ShapeDtypeStruct((N_X, N_Z + 1, F_OUT, BLOCK), bf16)
    keep, away = pl.pallas_call(
        backward_kernel,
        out_shape=(half, half),
        in_specs=[smem()] * 4 + [vmem()] * 2,
        out_specs=(vmem(), vmem()),
        scratch_shapes=[pltpu.VMEM((2 * HALF + 1, F_OUT, BLOCK), f32)],
        compiler_params=params,
        name="backward",
    )(tile_row, tile_col, tile_count, core, group, tile_values)
    recv = lax.ppermute(away, "c", [(0, 1), (1, 0)])
    by_core = pl.pallas_call(
        core_sum_kernel,
        out_shape=half,
        in_specs=[vmem()] * 2,
        out_specs=vmem(),
        compiler_params=params,
        name="core_sum",
    )(keep, recv)
    by_x = lax.all_to_all(by_core, "x", 0, 0)
    by_x = pl.pallas_call(
        x_sum_kernel,
        out_shape=jax.ShapeDtypeStruct((N_Z, 2, F_OUT, BLOCK), bf16),
        in_specs=[vmem()],
        out_specs=vmem(),
        compiler_params=params,
        name="x_sum",
    )(by_x)
    last = lax.all_to_all(by_x, "z", 0, 0)
    grad_features, grad_weight_t = pl.pallas_call(
        final_kernel,
        out_shape=(
            jax.ShapeDtypeStruct((BLOCK, F_IN), bf16),
            jax.ShapeDtypeStruct((F_OUT, F_IN), f32),
        ),
        in_specs=[vmem()] * 4,
        out_specs=(vmem(), vmem()),
        compiler_params=params,
        name="final",
    )(degrees, last, send, weight_t)
    return (mixed_t.T, grad_features, grad_weight_t.T)


def solution(mesh):
    devices = np.asarray(mesh.devices).reshape(N_Z, N_X, N_C, N_Y)
    fine = Mesh(devices, ("z", "x", "c", "y"))
    every = ("z", "x", "c", "y")
    in_specs = (
        P(every, None),
        P(every),
        P(every, None, None),
        P(every),
        P(every),
        P(every),
        P(),
        P(),
        P(every, None),
    )
    out_specs = (P(every, None), P(every, None), P())
    return jax.shard_map(shards, mesh=fine, in_specs=in_specs, out_specs=out_specs, check_vma=False)
```

```python
import numpy as np

import jax
import jax.numpy as jnp
from jax import lax
from jax.experimental import pallas as pl
from jax.experimental.pallas import tpu as pltpu
from jax.sharding import Mesh, PartitionSpec as P

N_Z, N_X, N_C, N_Y = 8, 4, 2, 8
BLOCK = 128
F_IN = 128
F_OUT = 64
CHUNK = 48
GROUP = 8
HALF = N_X * N_Z
VMEM_BYTES = 16 * 1024 * 1024
f32 = jnp.float32
bf16 = jnp.bfloat16


def scale_square(scales_ref):
    return jnp.transpose(jnp.broadcast_to(scales_ref[...], (BLOCK, BLOCK)))


def place_of(col, core):
    owner = lax.shift_right_logical(col, 3)
    z = lax.shift_right_logical(owner, 3)
    x = jnp.bitwise_and(lax.shift_right_logical(owner, 1), 3)
    other = jnp.bitwise_xor(jnp.bitwise_and(owner, 1), core)
    return other * HALF + x * N_Z + z


def start_kernel(scales_ref, features_ref, scaled_ref):
    scaled = (scale_square(scales_ref) * features_ref[...].astype(f32)).astype(bf16)
    scaled_ref[...] = jnp.broadcast_to(scaled[None], scaled_ref.shape)


def slot_copies(rows_ref, cols_ref, count_ref, rows, cols, count, sems):
    pairs = ((rows_ref, rows), (cols_ref, cols), (count_ref, count))
    return [pltpu.make_async_copy(src, dst, sems.at[i]) for i, (src, dst) in enumerate(pairs)]


def forward_kernel(
    rows_any, cols_any, count_any, own_ref, other_ref, values_ref, out_ref,
    rows_ref, cols_ref, count_ref, gathered, acc, sems,
):
    copies = slot_copies(rows_any, cols_any, count_any, rows_ref, cols_ref, count_ref, sems)
    for copy in copies:
        copy.start()
    core = lax.axis_index("c")
    gathered[0:HALF] = own_ref[...]
    gathered[HALF : 2 * HALF] = other_ref[...]
    acc[...] = jnp.zeros_like(acc)
    for copy in copies:
        copy.wait()
    count = count_ref[0]

    def chunk(i, carry):
        for g in range(0, CHUNK, GROUP):
            slots = [i * CHUNK + g + k for k in range(GROUP)]
            products = [
                jnp.dot(values_ref[t], gathered[place_of(cols_ref[t], core)], preferred_element_type=f32)
                for t in slots
            ]
            for t, product in zip(slots, products):
                row = jnp.where(t < count, jnp.bitwise_and(rows_ref[t], N_Y - 1), N_Y)
                acc[row] += product
        return carry

    lax.fori_loop(0, values_ref.shape[0] // CHUNK, chunk, 0)
    out_ref[...] = acc[0:N_Y].astype(bf16)


def middle_kernel(
    scales_ref, parts_ref, scaled_ref, weight_ref, bias_ref, cotangent_ref, mixed_ref, send_ref
):
    total = jnp.sum(parts_ref[...].astype(f32), axis=0) + scaled_ref[0].astype(f32)
    aggregated = (scale_square(scales_ref) * total).astype(bf16)
    preact = (
        lax.dot_general(weight_ref[...], aggregated, (((1,), (1,)), ((), ())), preferred_element_type=f32)
        + bias_ref[...]
    )
    gate = jax.nn.sigmoid(preact)
    mixed_ref[...] = (preact * gate).astype(bf16)
    slope = gate * (1.0 + preact * (1.0 - gate))
    grad_pre = (cotangent_ref[...].astype(f32) * slope).astype(bf16)
    lifted = (scales_ref[...] * grad_pre.astype(f32)).astype(bf16)
    weight_part = jnp.dot(grad_pre, aggregated, preferred_element_type=f32).astype(bf16)
    send_ref[:, 0] = jnp.broadcast_to(lifted[None], (N_Y, F_OUT, BLOCK))
    send_ref[:, 1] = jnp.broadcast_to(weight_part[None], (N_Y, F_OUT, F_IN))


def backward_kernel(
    rows_any, cols_any, count_any, group_ref, values_ref, mixed_ref, keep_ref, send_ref, mixed_any,
    rows_ref, cols_ref, count_ref, acc, sems,
):
    copies = slot_copies(rows_any, cols_any, count_any, rows_ref, cols_ref, count_ref, sems)
    mixed_copy = pltpu.make_async_copy(mixed_ref, mixed_any, sems.at[3])
    for copy in copies:
        copy.start()
    mixed_copy.start()
    core = lax.axis_index("c")
    acc[...] = jnp.zeros_like(acc)
    for copy in copies:
        copy.wait()
    count = count_ref[0]

    def chunk(i, carry):
        for g in range(0, CHUNK, GROUP):
            slots = [i * CHUNK + g + k for k in range(GROUP)]
            products = [
                jnp.dot(
                    group_ref[jnp.bitwise_and(rows_ref[t], N_Y - 1), 0],
                    values_ref[t],
                    preferred_element_type=f32,
                )
                for t in slots
            ]
            for t, product in zip(slots, products):
                place = jnp.where(t < count, place_of(cols_ref[t], core), 2 * HALF)
                acc[place] += product
        return carry

    lax.fori_loop(0, values_ref.shape[0] // CHUNK, chunk, 0)
    weight_part = jnp.sum(group_ref[:, 1].astype(f32), axis=0).astype(bf16)
    for x in range(N_X):
        keep_ref[x, 0:N_Z] = acc[x * N_Z : (x + 1) * N_Z].astype(bf16)
        send_ref[x, 0:N_Z] = acc[HALF + x * N_Z : HALF + (x + 1) * N_Z].astype(bf16)
        keep_ref[x, N_Z] = weight_part
        send_ref[x, N_Z] = weight_part
    mixed_copy.wait()


def core_sum_kernel(keep_ref, recv_ref, out_ref):
    out_ref[...] = (keep_ref[...].astype(f32) + recv_ref[...].astype(f32)).astype(bf16)


def x_sum_kernel(recv_ref, out_ref):
    total = jnp.sum(recv_ref[...].astype(f32), axis=0).astype(bf16)
    out_ref[:, 0] = total[0:N_Z]
    out_ref[:, 1] = jnp.broadcast_to(total[N_Z][None], (N_Z, F_OUT, F_IN))


def final_kernel(scales_ref, recv_ref, sent_ref, weight_ref, grad_features_ref, grad_weight_ref):
    total = jnp.sum(recv_ref[...].astype(f32), axis=0)
    grad_scaled = scales_ref[...] * (total[0] + sent_ref[0, 0].astype(f32))
    turned = jnp.transpose(grad_scaled).astype(bf16)
    grad_features_ref[...] = jnp.dot(turned, weight_ref[...], preferred_element_type=f32).astype(bf16)
    node_total = BLOCK * N_Z * N_X * N_C * N_Y
    grad_weight_ref[...] = total[1] * (1.0 / np.sqrt(node_total))


def vmem():
    return pl.BlockSpec(memory_space=pltpu.VMEM)


def anywhere():
    return pl.BlockSpec(memory_space=pl.ANY)


def shards(
    features, degrees, tile_values, tile_row, tile_col, tile_count, weight, out_bias, cotangent
):
    slots = tile_values.shape[0]
    scales = lax.rsqrt(degrees.astype(f32) + 1.0).reshape(1, BLOCK)
    weight_t = weight.T
    cotangent_t = cotangent.T
    bias = jnp.broadcast_to(out_bias.astype(f32)[:, None], (F_OUT, BLOCK))
    lists = [pltpu.SMEM((slots,), jnp.int32), pltpu.SMEM((slots,), jnp.int32), pltpu.SMEM((1,), jnp.int32)]
    params = pltpu.CompilerParams(vmem_limit_bytes=VMEM_BYTES)

    scaled = pl.pallas_call(
        start_kernel,
        out_shape=jax.ShapeDtypeStruct((N_Z, BLOCK, F_IN), bf16),
        in_specs=[vmem()] * 2,
        out_specs=vmem(),
        compiler_params=params,
        name="start",
    )(scales, features)
    by_z = lax.all_to_all(scaled, "z", 0, 0)
    by_xz = lax.all_to_all(jnp.broadcast_to(by_z[None], (N_X,) + by_z.shape), "x", 0, 0)
    own = by_xz.reshape(HALF, BLOCK, F_IN)
    other = lax.ppermute(own, "c", [(0, 1), (1, 0)])

    parts = pl.pallas_call(
        forward_kernel,
        out_shape=jax.ShapeDtypeStruct((N_Y, BLOCK, F_IN), bf16),
        in_specs=[anywhere()] * 3 + [vmem()] * 3,
        out_specs=vmem(),
        scratch_shapes=[
            *lists,
            pltpu.VMEM((2 * HALF, BLOCK, F_IN), bf16),
            pltpu.VMEM((N_Y + 1, BLOCK, F_IN), f32),
            pltpu.SemaphoreType.DMA((3,)),
        ],
        compiler_params=params,
        name="forward",
    )(tile_row, tile_col, tile_count, own, other, tile_values)
    parts = lax.all_to_all(parts, "y", 0, 0)

    mixed_here, send = pl.pallas_call(
        middle_kernel,
        out_shape=(
            jax.ShapeDtypeStruct((F_OUT, BLOCK), bf16),
            jax.ShapeDtypeStruct((N_Y, 2, F_OUT, BLOCK), bf16),
        ),
        in_specs=[vmem()] * 6,
        out_specs=(vmem(), vmem()),
        compiler_params=params,
        name="middle",
    )(scales, parts, scaled, weight_t, bias, cotangent_t)
    group = lax.all_to_all(send, "y", 0, 0)

    half = jax.ShapeDtypeStruct((N_X, N_Z + 1, F_OUT, BLOCK), bf16)
    keep, away, mixed_t = pl.pallas_call(
        backward_kernel,
        out_shape=(half, half, jax.ShapeDtypeStruct((F_OUT, BLOCK), bf16)),
        in_specs=[anywhere()] * 3 + [vmem()] * 3,
        out_specs=(vmem(), vmem(), anywhere()),
        scratch_shapes=[
            *lists,
            pltpu.VMEM((2 * HALF + 1, F_OUT, BLOCK), f32),
            pltpu.SemaphoreType.DMA((4,)),
        ],
        compiler_params=params,
        name="backward",
    )(tile_row, tile_col, tile_count, group, tile_values, mixed_here)
    recv = lax.ppermute(away, "c", [(0, 1), (1, 0)])
    by_core = pl.pallas_call(
        core_sum_kernel,
        out_shape=half,
        in_specs=[vmem()] * 2,
        out_specs=vmem(),
        compiler_params=params,
        name="core_sum",
    )(keep, recv)
    by_x = lax.all_to_all(by_core, "x", 0, 0)
    by_x = pl.pallas_call(
        x_sum_kernel,
        out_shape=jax.ShapeDtypeStruct((N_Z, 2, F_OUT, BLOCK), bf16),
        in_specs=[vmem()],
        out_specs=vmem(),
        compiler_params=params,
        name="x_sum",
    )(by_x)
    last = lax.all_to_all(by_x, "z", 0, 0)
    grad_features, grad_weight_t = pl.pallas_call(
        final_kernel,
        out_shape=(
            jax.ShapeDtypeStruct((BLOCK, F_IN), bf16),
            jax.ShapeDtypeStruct((F_OUT, F_IN), f32),
        ),
        in_specs=[vmem()] * 4,
        out_specs=(vmem(), vmem()),
        compiler_params=params,
        name="final",
    )(scales, last, send, weight_t)
    return (mixed_t.T, grad_features, grad_weight_t.T)


def solution(mesh):
    devices = np.asarray(mesh.devices).reshape(N_Z, N_X, N_C, N_Y)
    fine = Mesh(devices, ("z", "x", "c", "y"))
    every = ("z", "x", "c", "y")
    in_specs = (
        P(every, None),
        P(every),
        P(every, None, None),
        P(every),
        P(every),
        P(every),
        P(),
        P(),
        P(every, None),
    )
    out_specs = (P(every, None), P(every, None), P())
    return jax.shard_map(shards, mesh=fine, in_specs=in_specs, out_specs=out_specs, check_vma=False)
```

```python
import numpy as np

import jax
import jax.numpy as jnp
from jax import lax
from jax.experimental import pallas as pl
from jax.experimental.pallas import tpu as pltpu
from jax.sharding import Mesh, PartitionSpec as P

N_Z, N_X, N_C, N_Y = 8, 4, 2, 8
SIZES = (N_Z, N_X, N_C, N_Y)
BLOCK = 128
F_IN = 128
F_OUT = 64
CHUNK = 48
GROUP = 8
HALF = N_X * N_Z
VMEM_BYTES = 16 * 1024 * 1024
f32 = jnp.float32
bf16 = jnp.bfloat16


def scale_square(scales_ref):
    return jnp.transpose(jnp.broadcast_to(scales_ref[...], (BLOCK, BLOCK)))


def own_core():
    return jnp.bitwise_and(lax.shift_right_logical(lax.axis_index("d"), 3), 1)


def place_of(col, core):
    owner = lax.shift_right_logical(col, 3)
    z = lax.shift_right_logical(owner, 3)
    x = jnp.bitwise_and(lax.shift_right_logical(owner, 1), 3)
    other = jnp.bitwise_xor(jnp.bitwise_and(owner, 1), core)
    return other * HALF + (N_X - 1 - x) * N_Z + (N_Z - 1 - z)


def place_in_group(row):
    return N_Y - 1 - jnp.bitwise_and(row, N_Y - 1)


def exchange(blocks, axis):
    numbers = np.moveaxis(np.arange(np.prod(SIZES)).reshape(SIZES), axis, -1)
    groups = numbers.reshape(-1, SIZES[axis])[:, ::-1].tolist()
    return lax.all_to_all(blocks, "d", 0, 0, axis_index_groups=groups)


def swap_cores(blocks):
    return lax.ppermute(blocks, "d", [(i, i ^ N_Y) for i in range(np.prod(SIZES))])


def start_kernel(scales_ref, features_ref, scaled_ref):
    scaled = (scale_square(scales_ref) * features_ref[...].astype(f32)).astype(bf16)
    scaled_ref[...] = jnp.broadcast_to(scaled[None], scaled_ref.shape)


def slot_copies(rows_ref, cols_ref, count_ref, rows, cols, count, sems):
    pairs = ((rows_ref, rows), (cols_ref, cols), (count_ref, count))
    return [pltpu.make_async_copy(src, dst, sems.at[i]) for i, (src, dst) in enumerate(pairs)]


def forward_kernel(
    rows_any, cols_any, count_any, own_ref, other_ref, values_ref, out_ref,
    rows_ref, cols_ref, count_ref, gathered, acc, sems,
):
    copies = slot_copies(rows_any, cols_any, count_any, rows_ref, cols_ref, count_ref, sems)
    for copy in copies:
        copy.start()
    core = own_core()
    gathered[0:HALF] = own_ref[...]
    gathered[HALF : 2 * HALF] = other_ref[...]
    acc[...] = jnp.zeros_like(acc)
    for copy in copies:
        copy.wait()
    count = count_ref[0]

    def chunk(i, carry):
        for g in range(0, CHUNK, GROUP):
            slots = [i * CHUNK + g + k for k in range(GROUP)]
            products = [
                jnp.dot(values_ref[t], gathered[place_of(cols_ref[t], core)], preferred_element_type=f32)
                for t in slots
            ]
            for t, product in zip(slots, products):
                row = jnp.where(t < count, place_in_group(rows_ref[t]), N_Y)
                acc[row] += product
        return carry

    lax.fori_loop(0, values_ref.shape[0] // CHUNK, chunk, 0)
    out_ref[...] = acc[0:N_Y].astype(bf16)


def middle_kernel(
    scales_ref, parts_ref, scaled_ref, weight_ref, bias_ref, cotangent_ref, mixed_ref, send_ref
):
    total = jnp.sum(parts_ref[...].astype(f32), axis=0) + scaled_ref[0].astype(f32)
    aggregated = (scale_square(scales_ref) * total).astype(bf16)
    preact = (
        lax.dot_general(weight_ref[...], aggregated, (((1,), (1,)), ((), ())), preferred_element_type=f32)
        + bias_ref[...]
    )
    gate = jax.nn.sigmoid(preact)
    mixed_ref[...] = (preact * gate).astype(bf16)
    slope = gate * (1.0 + preact * (1.0 - gate))
    grad_pre = (cotangent_ref[...].astype(f32) * slope).astype(bf16)
    lifted = (scales_ref[...] * grad_pre.astype(f32)).astype(bf16)
    weight_part = jnp.dot(grad_pre, aggregated, preferred_element_type=f32).astype(bf16)
    send_ref[:, 0] = jnp.broadcast_to(lifted[None], (N_Y, F_OUT, BLOCK))
    send_ref[:, 1] = jnp.broadcast_to(weight_part[None], (N_Y, F_OUT, F_IN))


def backward_kernel(
    rows_any, cols_any, count_any, group_ref, values_ref, mixed_ref, keep_ref, send_ref, mixed_any,
    rows_ref, cols_ref, count_ref, acc, sems,
):
    copies = slot_copies(rows_any, cols_any, count_any, rows_ref, cols_ref, count_ref, sems)
    mixed_copy = pltpu.make_async_copy(mixed_ref, mixed_any, sems.at[3])
    for copy in copies:
        copy.start()
    mixed_copy.start()
    core = own_core()
    acc[...] = jnp.zeros_like(acc)
    for copy in copies:
        copy.wait()
    count = count_ref[0]

    def chunk(i, carry):
        for g in range(0, CHUNK, GROUP):
            slots = [i * CHUNK + g + k for k in range(GROUP)]
            products = [
                jnp.dot(
                    group_ref[place_in_group(rows_ref[t]), 0],
                    values_ref[t],
                    preferred_element_type=f32,
                )
                for t in slots
            ]
            for t, product in zip(slots, products):
                place = jnp.where(t < count, place_of(cols_ref[t], core), 2 * HALF)
                acc[place] += product
        return carry

    lax.fori_loop(0, values_ref.shape[0] // CHUNK, chunk, 0)
    weight_part = jnp.sum(group_ref[:, 1].astype(f32), axis=0).astype(bf16)
    for x in range(N_X):
        keep_ref[x, 0:N_Z] = acc[x * N_Z : (x + 1) * N_Z].astype(bf16)
        send_ref[x, 0:N_Z] = acc[HALF + x * N_Z : HALF + (x + 1) * N_Z].astype(bf16)
        keep_ref[x, N_Z] = weight_part
        send_ref[x, N_Z] = weight_part
    mixed_copy.wait()


def core_sum_kernel(keep_ref, recv_ref, out_ref):
    out_ref[...] = (keep_ref[...].astype(f32) + recv_ref[...].astype(f32)).astype(bf16)


def x_sum_kernel(recv_ref, out_ref):
    total = jnp.sum(recv_ref[...].astype(f32), axis=0).astype(bf16)
    out_ref[:, 0] = total[0:N_Z]
    out_ref[:, 1] = jnp.broadcast_to(total[N_Z][None], (N_Z, F_OUT, F_IN))


def final_kernel(scales_ref, recv_ref, sent_ref, weight_ref, grad_features_ref, grad_weight_ref):
    total = jnp.sum(recv_ref[...].astype(f32), axis=0)
    grad_scaled = scales_ref[...] * (total[0] + sent_ref[0, 0].astype(f32))
    turned = jnp.transpose(grad_scaled).astype(bf16)
    grad_features_ref[...] = jnp.dot(turned, weight_ref[...], preferred_element_type=f32).astype(bf16)
    node_total = BLOCK * N_Z * N_X * N_C * N_Y
    grad_weight_ref[...] = total[1] * (1.0 / np.sqrt(node_total))


def vmem():
    return pl.BlockSpec(memory_space=pltpu.VMEM)


def anywhere():
    return pl.BlockSpec(memory_space=pl.ANY)


def shards(
    features, degrees, tile_values, tile_row, tile_col, tile_count, weight, out_bias, cotangent
):
    slots = tile_values.shape[0]
    scales = lax.rsqrt(degrees.astype(f32) + 1.0).reshape(1, BLOCK)
    weight_t = weight.T
    cotangent_t = cotangent.T
    bias = jnp.broadcast_to(out_bias.astype(f32)[:, None], (F_OUT, BLOCK))
    lists = [pltpu.SMEM((slots,), jnp.int32), pltpu.SMEM((slots,), jnp.int32), pltpu.SMEM((1,), jnp.int32)]
    params = pltpu.CompilerParams(vmem_limit_bytes=VMEM_BYTES)

    scaled = pl.pallas_call(
        start_kernel,
        out_shape=jax.ShapeDtypeStruct((N_Z, BLOCK, F_IN), bf16),
        in_specs=[vmem()] * 2,
        out_specs=vmem(),
        compiler_params=params,
        name="start",
    )(scales, features)
    by_z = exchange(scaled, 0)
    by_xz = exchange(jnp.broadcast_to(by_z[None], (N_X,) + by_z.shape), 1)
    own = by_xz.reshape(HALF, BLOCK, F_IN)
    other = swap_cores(own)

    parts = pl.pallas_call(
        forward_kernel,
        out_shape=jax.ShapeDtypeStruct((N_Y, BLOCK, F_IN), bf16),
        in_specs=[anywhere()] * 3 + [vmem()] * 3,
        out_specs=vmem(),
        scratch_shapes=[
            *lists,
            pltpu.VMEM((2 * HALF, BLOCK, F_IN), bf16),
            pltpu.VMEM((N_Y + 1, BLOCK, F_IN), f32),
            pltpu.SemaphoreType.DMA((3,)),
        ],
        compiler_params=params,
        name="forward",
    )(tile_row, tile_col, tile_count, own, other, tile_values)
    parts = exchange(parts, 3)

    mixed_here, send = pl.pallas_call(
        middle_kernel,
        out_shape=(
            jax.ShapeDtypeStruct((F_OUT, BLOCK), bf16),
            jax.ShapeDtypeStruct((N_Y, 2, F_OUT, BLOCK), bf16),
        ),
        in_specs=[vmem()] * 6,
        out_specs=(vmem(), vmem()),
        compiler_params=params,
        name="middle",
    )(scales, parts, scaled, weight_t, bias, cotangent_t)
    group = exchange(send, 3)

    half = jax.ShapeDtypeStruct((N_X, N_Z + 1, F_OUT, BLOCK), bf16)
    keep, away, mixed_t = pl.pallas_call(
        backward_kernel,
        out_shape=(half, half, jax.ShapeDtypeStruct((F_OUT, BLOCK), bf16)),
        in_specs=[anywhere()] * 3 + [vmem()] * 3,
        out_specs=(vmem(), vmem(), anywhere()),
        scratch_shapes=[
            *lists,
            pltpu.VMEM((2 * HALF + 1, F_OUT, BLOCK), f32),
            pltpu.SemaphoreType.DMA((4,)),
        ],
        compiler_params=params,
        name="backward",
    )(tile_row, tile_col, tile_count, group, tile_values, mixed_here)
    recv = swap_cores(away)
    by_core = pl.pallas_call(
        core_sum_kernel,
        out_shape=half,
        in_specs=[vmem()] * 2,
        out_specs=vmem(),
        compiler_params=params,
        name="core_sum",
    )(keep, recv)
    by_x = exchange(by_core, 1)
    by_x = pl.pallas_call(
        x_sum_kernel,
        out_shape=jax.ShapeDtypeStruct((N_Z, 2, F_OUT, BLOCK), bf16),
        in_specs=[vmem()],
        out_specs=vmem(),
        compiler_params=params,
        name="x_sum",
    )(by_x)
    last = exchange(by_x, 0)
    grad_features, grad_weight_t = pl.pallas_call(
        final_kernel,
        out_shape=(
            jax.ShapeDtypeStruct((BLOCK, F_IN), bf16),
            jax.ShapeDtypeStruct((F_OUT, F_IN), f32),
        ),
        in_specs=[vmem()] * 4,
        out_specs=(vmem(), vmem()),
        compiler_params=params,
        name="final",
    )(scales, last, send, weight_t)
    return (mixed_t.T, grad_features, grad_weight_t.T)


def solution(mesh):
    line = Mesh(np.asarray(mesh.devices).reshape(-1), ("d",))
    in_specs = (P("d", None), P("d"), P("d", None, None), P("d"), P("d"), P("d"), P(), P(), P("d", None))
    out_specs = (P("d", None), P("d", None), P())
    return jax.shard_map(shards, mesh=line, in_specs=in_specs, out_specs=out_specs, check_vma=False)
```

```python
import numpy as np

import jax
import jax.numpy as jnp
from jax import lax
from jax.experimental import pallas as pl
from jax.experimental.pallas import tpu as pltpu
from jax.sharding import Mesh, PartitionSpec as P

N_Z, N_X, N_C, N_Y = 8, 4, 2, 8
SIZES = (N_Z, N_X, N_C, N_Y)
BLOCK = 128
F_IN = 128
F_OUT = 64
CHUNK = 48
GROUP = 8
HALF = N_X * N_Z
VMEM_BYTES = 16 * 1024 * 1024
f32 = jnp.float32
bf16 = jnp.bfloat16


def scale_square(scales_ref):
    return jnp.transpose(jnp.broadcast_to(scales_ref[...], (BLOCK, BLOCK)))


def own_core():
    return jnp.bitwise_and(lax.shift_right_logical(lax.axis_index("d"), 3), 1)


def turned(number):
    low, high = jnp.bitwise_and(number, 1), lax.shift_right_logical(number, 2)
    return lax.shift_left(low, 2) + jnp.bitwise_and(number, 2) + high


def place_of(col, core):
    owner = lax.shift_right_logical(col, 3)
    z = lax.shift_right_logical(owner, 3)
    x = jnp.bitwise_and(lax.shift_right_logical(owner, 1), 3)
    half = jnp.bitwise_and(owner, 1)
    other = jnp.bitwise_xor(half, core)
    return other * HALF + (N_X - 1 - x) * N_Z + turned(jnp.bitwise_xor(jnp.bitwise_xor(z, half), N_Z - 1))


def place_in_group(row, core):
    return turned(jnp.bitwise_xor(jnp.bitwise_xor(jnp.bitwise_and(row, N_Y - 1), core), N_Y - 1))


def exchange(blocks, axis):
    size = SIZES[axis]
    numbers = np.moveaxis(np.arange(np.prod(SIZES)).reshape(SIZES), axis, -1)
    cores = numbers[..., 0].reshape(-1) // N_Y % N_C
    groups = []
    for group, core in zip(numbers.reshape(-1, size), cores):
        order = [k ^ 7 ^ int(core) for k in (0, 4, 2, 6, 1, 5, 3, 7)] if size == 8 else range(size)[::-1]
        groups.append([int(group[k]) for k in order])
    return lax.all_to_all(blocks, "d", 0, 0, axis_index_groups=groups)


def swap_cores(blocks):
    return lax.ppermute(blocks, "d", [(i, i ^ N_Y) for i in range(np.prod(SIZES))])


def start_kernel(scales_ref, features_ref, scaled_ref):
    scaled = (scale_square(scales_ref) * features_ref[...].astype(f32)).astype(bf16)
    scaled_ref[...] = jnp.broadcast_to(scaled[None], scaled_ref.shape)


def slot_copies(rows_ref, cols_ref, count_ref, rows, cols, count, sems):
    pairs = ((rows_ref, rows), (cols_ref, cols), (count_ref, count))
    return [pltpu.make_async_copy(src, dst, sems.at[i]) for i, (src, dst) in enumerate(pairs)]


def forward_kernel(
    rows_any, cols_any, count_any, own_ref, other_ref, values_ref, out_ref,
    rows_ref, cols_ref, count_ref, gathered, acc, sems,
):
    copies = slot_copies(rows_any, cols_any, count_any, rows_ref, cols_ref, count_ref, sems)
    for copy in copies:
        copy.start()
    core = own_core()
    gathered[0:HALF] = own_ref[...]
    gathered[HALF : 2 * HALF] = other_ref[...]
    acc[...] = jnp.zeros_like(acc)
    for copy in copies:
        copy.wait()
    count = count_ref[0]

    def chunk(i, carry):
        for g in range(0, CHUNK, GROUP):
            slots = [i * CHUNK + g + k for k in range(GROUP)]
            products = [
                jnp.dot(values_ref[t], gathered[place_of(cols_ref[t], core)], preferred_element_type=f32)
                for t in slots
            ]
            for t, product in zip(slots, products):
                row = jnp.where(t < count, place_in_group(rows_ref[t], core), N_Y)
                acc[row] += product
        return carry

    lax.fori_loop(0, values_ref.shape[0] // CHUNK, chunk, 0)
    out_ref[...] = acc[0:N_Y].astype(bf16)


def middle_kernel(
    scales_ref, parts_ref, scaled_ref, weight_ref, bias_ref, cotangent_ref, mixed_ref, send_ref
):
    total = jnp.sum(parts_ref[...].astype(f32), axis=0) + scaled_ref[0].astype(f32)
    aggregated = (scale_square(scales_ref) * total).astype(bf16)
    preact = (
        lax.dot_general(weight_ref[...], aggregated, (((1,), (1,)), ((), ())), preferred_element_type=f32)
        + bias_ref[...]
    )
    gate = jax.nn.sigmoid(preact)
    mixed_ref[...] = (preact * gate).astype(bf16)
    slope = gate * (1.0 + preact * (1.0 - gate))
    grad_pre = (cotangent_ref[...].astype(f32) * slope).astype(bf16)
    lifted = (scales_ref[...] * grad_pre.astype(f32)).astype(bf16)
    weight_part = jnp.dot(grad_pre, aggregated, preferred_element_type=f32).astype(bf16)
    send_ref[:, 0] = jnp.broadcast_to(lifted[None], (N_Y, F_OUT, BLOCK))
    send_ref[:, 1] = jnp.broadcast_to(weight_part[None], (N_Y, F_OUT, F_IN))


def backward_kernel(
    rows_any, cols_any, count_any, group_ref, values_ref, mixed_ref, keep_ref, send_ref, mixed_any,
    rows_ref, cols_ref, count_ref, acc, sems,
):
    copies = slot_copies(rows_any, cols_any, count_any, rows_ref, cols_ref, count_ref, sems)
    mixed_copy = pltpu.make_async_copy(mixed_ref, mixed_any, sems.at[3])
    for copy in copies:
        copy.start()
    mixed_copy.start()
    core = own_core()
    acc[...] = jnp.zeros_like(acc)
    for copy in copies:
        copy.wait()
    count = count_ref[0]

    def chunk(i, carry):
        for g in range(0, CHUNK, GROUP):
            slots = [i * CHUNK + g + k for k in range(GROUP)]
            products = [
                jnp.dot(
                    group_ref[place_in_group(rows_ref[t], core), 0],
                    values_ref[t],
                    preferred_element_type=f32,
                )
                for t in slots
            ]
            for t, product in zip(slots, products):
                place = jnp.where(t < count, place_of(cols_ref[t], core), 2 * HALF)
                acc[place] += product
        return carry

    lax.fori_loop(0, values_ref.shape[0] // CHUNK, chunk, 0)
    weight_part = jnp.sum(group_ref[:, 1].astype(f32), axis=0).astype(bf16)
    for x in range(N_X):
        keep_ref[x, 0:N_Z] = acc[x * N_Z : (x + 1) * N_Z].astype(bf16)
        send_ref[x, 0:N_Z] = acc[HALF + x * N_Z : HALF + (x + 1) * N_Z].astype(bf16)
        keep_ref[x, N_Z] = weight_part
        send_ref[x, N_Z] = weight_part
    mixed_copy.wait()


def core_sum_kernel(keep_ref, recv_ref, out_ref):
    out_ref[...] = (keep_ref[...].astype(f32) + recv_ref[...].astype(f32)).astype(bf16)


def x_sum_kernel(recv_ref, out_ref):
    total = jnp.sum(recv_ref[...].astype(f32), axis=0).astype(bf16)
    out_ref[:, 0] = total[0:N_Z]
    out_ref[:, 1] = jnp.broadcast_to(total[N_Z][None], (N_Z, F_OUT, F_IN))


def final_kernel(scales_ref, recv_ref, sent_ref, weight_ref, grad_features_ref, grad_weight_ref):
    total = jnp.sum(recv_ref[...].astype(f32), axis=0)
    grad_scaled = scales_ref[...] * (total[0] + sent_ref[0, 0].astype(f32))
    turned = jnp.transpose(grad_scaled).astype(bf16)
    grad_features_ref[...] = jnp.dot(turned, weight_ref[...], preferred_element_type=f32).astype(bf16)
    node_total = BLOCK * N_Z * N_X * N_C * N_Y
    grad_weight_ref[...] = total[1] * (1.0 / np.sqrt(node_total))


def vmem():
    return pl.BlockSpec(memory_space=pltpu.VMEM)


def anywhere():
    return pl.BlockSpec(memory_space=pl.ANY)


def shards(
    features, degrees, tile_values, tile_row, tile_col, tile_count, weight, out_bias, cotangent
):
    slots = tile_values.shape[0]
    scales = lax.rsqrt(degrees.astype(f32) + 1.0).reshape(1, BLOCK)
    weight_t = weight.T
    cotangent_t = cotangent.T
    bias = jnp.broadcast_to(out_bias.astype(f32)[:, None], (F_OUT, BLOCK))
    lists = [pltpu.SMEM((slots,), jnp.int32), pltpu.SMEM((slots,), jnp.int32), pltpu.SMEM((1,), jnp.int32)]
    params = pltpu.CompilerParams(vmem_limit_bytes=VMEM_BYTES)

    scaled = pl.pallas_call(
        start_kernel,
        out_shape=jax.ShapeDtypeStruct((N_Z, BLOCK, F_IN), bf16),
        in_specs=[vmem()] * 2,
        out_specs=vmem(),
        compiler_params=params,
        name="start",
    )(scales, features)
    by_z = exchange(scaled, 0)
    by_xz = exchange(jnp.broadcast_to(by_z[None], (N_X,) + by_z.shape), 1)
    own = by_xz.reshape(HALF, BLOCK, F_IN)
    other = swap_cores(own)

    parts = pl.pallas_call(
        forward_kernel,
        out_shape=jax.ShapeDtypeStruct((N_Y, BLOCK, F_IN), bf16),
        in_specs=[anywhere()] * 3 + [vmem()] * 3,
        out_specs=vmem(),
        scratch_shapes=[
            *lists,
            pltpu.VMEM((2 * HALF, BLOCK, F_IN), bf16),
            pltpu.VMEM((N_Y + 1, BLOCK, F_IN), f32),
            pltpu.SemaphoreType.DMA((3,)),
        ],
        compiler_params=params,
        name="forward",
    )(tile_row, tile_col, tile_count, own, other, tile_values)
    parts = exchange(parts, 3)

    mixed_here, send = pl.pallas_call(
        middle_kernel,
        out_shape=(
            jax.ShapeDtypeStruct((F_OUT, BLOCK), bf16),
            jax.ShapeDtypeStruct((N_Y, 2, F_OUT, BLOCK), bf16),
        ),
        in_specs=[vmem()] * 6,
        out_specs=(vmem(), vmem()),
        compiler_params=params,
        name="middle",
    )(scales, parts, scaled, weight_t, bias, cotangent_t)
    group = exchange(send, 3)

    half = jax.ShapeDtypeStruct((N_X, N_Z + 1, F_OUT, BLOCK), bf16)
    keep, away, mixed_t = pl.pallas_call(
        backward_kernel,
        out_shape=(half, half, jax.ShapeDtypeStruct((F_OUT, BLOCK), bf16)),
        in_specs=[anywhere()] * 3 + [vmem()] * 3,
        out_specs=(vmem(), vmem(), anywhere()),
        scratch_shapes=[
            *lists,
            pltpu.VMEM((2 * HALF + 1, F_OUT, BLOCK), f32),
            pltpu.SemaphoreType.DMA((4,)),
        ],
        compiler_params=params,
        name="backward",
    )(tile_row, tile_col, tile_count, group, tile_values, mixed_here)
    recv = swap_cores(away)
    by_core = pl.pallas_call(
        core_sum_kernel,
        out_shape=half,
        in_specs=[vmem()] * 2,
        out_specs=vmem(),
        compiler_params=params,
        name="core_sum",
    )(keep, recv)
    by_x = exchange(by_core, 1)
    by_x = pl.pallas_call(
        x_sum_kernel,
        out_shape=jax.ShapeDtypeStruct((N_Z, 2, F_OUT, BLOCK), bf16),
        in_specs=[vmem()],
        out_specs=vmem(),
        compiler_params=params,
        name="x_sum",
    )(by_x)
    last = exchange(by_x, 0)
    grad_features, grad_weight_t = pl.pallas_call(
        final_kernel,
        out_shape=(
            jax.ShapeDtypeStruct((BLOCK, F_IN), bf16),
            jax.ShapeDtypeStruct((F_OUT, F_IN), f32),
        ),
        in_specs=[vmem()] * 4,
        out_specs=(vmem(), vmem()),
        compiler_params=params,
        name="final",
    )(scales, last, send, weight_t)
    return (mixed_t.T, grad_features, grad_weight_t.T)


def solution(mesh):
    line = Mesh(np.asarray(mesh.devices).reshape(-1), ("d",))
    in_specs = (P("d", None), P("d"), P("d", None, None), P("d"), P("d"), P("d"), P(), P(), P("d", None))
    out_specs = (P("d", None), P("d", None), P())
    return jax.shard_map(shards, mesh=line, in_specs=in_specs, out_specs=out_specs, check_vma=False)
```

```python
import numpy as np

import jax
import jax.numpy as jnp
from jax import lax
from jax.experimental import pallas as pl
from jax.experimental.pallas import tpu as pltpu
from jax.sharding import Mesh, PartitionSpec as P

N_Z, N_X, N_C, N_Y = 8, 4, 2, 8
SIZES = (N_Z, N_X, N_C, N_Y)
BLOCK = 128
F_IN = 128
F_OUT = 64
CHUNK = 48
GROUP = 8
HALF = N_X * N_Z
OPPOSITE = N_Z // 2 * N_X + N_X // 2
VMEM_BYTES = 16 * 1024 * 1024
f32 = jnp.float32
bf16 = jnp.bfloat16


def scale_square(scales_ref):
    return jnp.transpose(jnp.broadcast_to(scales_ref[...], (BLOCK, BLOCK)))


def own_core():
    return jnp.bitwise_and(lax.shift_right_logical(lax.axis_index("d"), 3), 1)


def turned(number):
    low, high = jnp.bitwise_and(number, 1), lax.shift_right_logical(number, 2)
    return lax.shift_left(low, 2) + jnp.bitwise_and(number, 2) + high


def place_gathered(col, core):
    owner = lax.shift_right_logical(col, 3)
    half = jnp.bitwise_and(owner, 1)
    chip = lax.shift_right_logical(owner, 1)
    return jnp.bitwise_xor(half, core) * HALF + jnp.bitwise_xor(chip, half * OPPOSITE)


def place_of(col, core):
    owner = lax.shift_right_logical(col, 3)
    z = lax.shift_right_logical(owner, 3)
    x = jnp.bitwise_and(lax.shift_right_logical(owner, 1), 3)
    half = jnp.bitwise_and(owner, 1)
    other = jnp.bitwise_xor(half, core)
    return other * HALF + (N_X - 1 - x) * N_Z + turned(jnp.bitwise_xor(jnp.bitwise_xor(z, half), N_Z - 1))


def place_in_group(row, core):
    return turned(jnp.bitwise_xor(jnp.bitwise_xor(jnp.bitwise_and(row, N_Y - 1), core), N_Y - 1))


def exchange(blocks, axis):
    size = SIZES[axis]
    numbers = np.moveaxis(np.arange(np.prod(SIZES)).reshape(SIZES), axis, -1)
    cores = numbers[..., 0].reshape(-1) // N_Y % N_C
    groups = []
    for group, core in zip(numbers.reshape(-1, size), cores):
        order = [k ^ 7 ^ int(core) for k in (0, 4, 2, 6, 1, 5, 3, 7)] if size == 8 else range(size)[::-1]
        groups.append([int(group[k]) for k in order])
    return lax.all_to_all(blocks, "d", 0, 0, axis_index_groups=groups)


def gather_plane(copies):
    numbers = np.arange(np.prod(SIZES)).reshape(HALF, N_C, N_Y)
    groups = [numbers[np.arange(HALF) ^ (c * OPPOSITE), c, y].tolist() for c in range(N_C) for y in range(N_Y)]
    return lax.all_to_all(copies, "d", 0, 0, axis_index_groups=groups)


def swap_cores(blocks):
    return lax.ppermute(blocks, "d", [(i, i ^ N_Y) for i in range(np.prod(SIZES))])


def start_kernel(scales_ref, features_ref, scaled_ref):
    scaled = (scale_square(scales_ref) * features_ref[...].astype(f32)).astype(bf16)
    scaled_ref[...] = jnp.broadcast_to(scaled[None], scaled_ref.shape)


def slot_copies(rows_ref, cols_ref, count_ref, rows, cols, count, sems):
    pairs = ((rows_ref, rows), (cols_ref, cols), (count_ref, count))
    return [pltpu.make_async_copy(src, dst, sems.at[i]) for i, (src, dst) in enumerate(pairs)]


def forward_kernel(
    rows_any, cols_any, count_any, own_ref, other_ref, values_ref, out_ref,
    rows_ref, cols_ref, count_ref, gathered, acc, sems,
):
    copies = slot_copies(rows_any, cols_any, count_any, rows_ref, cols_ref, count_ref, sems)
    for copy in copies:
        copy.start()
    core = own_core()
    gathered[0:HALF] = own_ref[...]
    gathered[HALF : 2 * HALF] = other_ref[...]
    acc[...] = jnp.zeros_like(acc)
    for copy in copies:
        copy.wait()
    count = count_ref[0]

    def chunk(i, carry):
        for g in range(0, CHUNK, GROUP):
            slots = [i * CHUNK + g + k for k in range(GROUP)]
            products = [
                jnp.dot(values_ref[t], gathered[place_gathered(cols_ref[t], core)], preferred_element_type=f32)
                for t in slots
            ]
            for t, product in zip(slots, products):
                row = jnp.where(t < count, place_in_group(rows_ref[t], core), N_Y)
                acc[row] += product
        return carry

    lax.fori_loop(0, values_ref.shape[0] // CHUNK, chunk, 0)
    out_ref[...] = acc[0:N_Y].astype(bf16)


def middle_kernel(
    scales_ref, parts_ref, scaled_ref, weight_ref, bias_ref, cotangent_ref, mixed_ref, send_ref
):
    total = jnp.sum(parts_ref[...].astype(f32), axis=0) + scaled_ref[0].astype(f32)
    aggregated = (scale_square(scales_ref) * total).astype(bf16)
    preact = (
        lax.dot_general(weight_ref[...], aggregated, (((1,), (1,)), ((), ())), preferred_element_type=f32)
        + bias_ref[...]
    )
    gate = jax.nn.sigmoid(preact)
    mixed_ref[...] = (preact * gate).astype(bf16)
    slope = gate * (1.0 + preact * (1.0 - gate))
    grad_pre = (cotangent_ref[...].astype(f32) * slope).astype(bf16)
    lifted = (scales_ref[...] * grad_pre.astype(f32)).astype(bf16)
    weight_part = jnp.dot(grad_pre, aggregated, preferred_element_type=f32).astype(bf16)
    send_ref[:, 0] = jnp.broadcast_to(lifted[None], (N_Y, F_OUT, BLOCK))
    send_ref[:, 1] = jnp.broadcast_to(weight_part[None], (N_Y, F_OUT, F_IN))


def backward_kernel(
    rows_any, cols_any, count_any, group_ref, values_ref, mixed_ref, keep_ref, send_ref, mixed_any,
    rows_ref, cols_ref, count_ref, acc, sems,
):
    copies = slot_copies(rows_any, cols_any, count_any, rows_ref, cols_ref, count_ref, sems)
    mixed_copy = pltpu.make_async_copy(mixed_ref, mixed_any, sems.at[3])
    for copy in copies:
        copy.start()
    mixed_copy.start()
    core = own_core()
    acc[...] = jnp.zeros_like(acc)
    for copy in copies:
        copy.wait()
    count = count_ref[0]

    def chunk(i, carry):
        for g in range(0, CHUNK, GROUP):
            slots = [i * CHUNK + g + k for k in range(GROUP)]
            products = [
                jnp.dot(
                    group_ref[place_in_group(rows_ref[t], core), 0],
                    values_ref[t],
                    preferred_element_type=f32,
                )
                for t in slots
            ]
            for t, product in zip(slots, products):
                place = jnp.where(t < count, place_of(cols_ref[t], core), 2 * HALF)
                acc[place] += product
        return carry

    lax.fori_loop(0, values_ref.shape[0] // CHUNK, chunk, 0)
    weight_part = jnp.sum(group_ref[:, 1].astype(f32), axis=0).astype(bf16)
    for x in range(N_X):
        keep_ref[x, 0:N_Z] = acc[x * N_Z : (x + 1) * N_Z].astype(bf16)
        send_ref[x, 0:N_Z] = acc[HALF + x * N_Z : HALF + (x + 1) * N_Z].astype(bf16)
        keep_ref[x, N_Z] = weight_part
        send_ref[x, N_Z] = weight_part
    mixed_copy.wait()


def core_sum_kernel(keep_ref, recv_ref, out_ref):
    out_ref[...] = (keep_ref[...].astype(f32) + recv_ref[...].astype(f32)).astype(bf16)


def x_sum_kernel(recv_ref, out_ref):
    total = jnp.sum(recv_ref[...].astype(f32), axis=0).astype(bf16)
    out_ref[:, 0] = total[0:N_Z]
    out_ref[:, 1] = jnp.broadcast_to(total[N_Z][None], (N_Z, F_OUT, F_IN))


def final_kernel(scales_ref, recv_ref, sent_ref, weight_ref, grad_features_ref, grad_weight_ref):
    total = jnp.sum(recv_ref[...].astype(f32), axis=0)
    grad_scaled = scales_ref[...] * (total[0] + sent_ref[0, 0].astype(f32))
    turned = jnp.transpose(grad_scaled).astype(bf16)
    grad_features_ref[...] = jnp.dot(turned, weight_ref[...], preferred_element_type=f32).astype(bf16)
    node_total = BLOCK * N_Z * N_X * N_C * N_Y
    grad_weight_ref[...] = total[1] * (1.0 / np.sqrt(node_total))


def vmem():
    return pl.BlockSpec(memory_space=pltpu.VMEM)


def anywhere():
    return pl.BlockSpec(memory_space=pl.ANY)


def shards(
    features, degrees, tile_values, tile_row, tile_col, tile_count, weight, out_bias, cotangent
):
    slots = tile_values.shape[0]
    scales = lax.rsqrt(degrees.astype(f32) + 1.0).reshape(1, BLOCK)
    weight_t = weight.T
    cotangent_t = cotangent.T
    bias = jnp.broadcast_to(out_bias.astype(f32)[:, None], (F_OUT, BLOCK))
    lists = [pltpu.SMEM((slots,), jnp.int32), pltpu.SMEM((slots,), jnp.int32), pltpu.SMEM((1,), jnp.int32)]
    params = pltpu.CompilerParams(vmem_limit_bytes=VMEM_BYTES)

    scaled = pl.pallas_call(
        start_kernel,
        out_shape=jax.ShapeDtypeStruct((HALF, BLOCK, F_IN), bf16),
        in_specs=[vmem()] * 2,
        out_specs=vmem(),
        compiler_params=params,
        name="start",
    )(scales, features)
    own = gather_plane(scaled)
    other = swap_cores(own)

    parts = pl.pallas_call(
        forward_kernel,
        out_shape=jax.ShapeDtypeStruct((N_Y, BLOCK, F_IN), bf16),
        in_specs=[anywhere()] * 3 + [vmem()] * 3,
        out_specs=vmem(),
        scratch_shapes=[
            *lists,
            pltpu.VMEM((2 * HALF, BLOCK, F_IN), bf16),
            pltpu.VMEM((N_Y + 1, BLOCK, F_IN), f32),
            pltpu.SemaphoreType.DMA((3,)),
        ],
        compiler_params=params,
        name="forward",
    )(tile_row, tile_col, tile_count, own, other, tile_values)
    parts = exchange(parts, 3)

    mixed_here, send = pl.pallas_call(
        middle_kernel,
        out_shape=(
            jax.ShapeDtypeStruct((F_OUT, BLOCK), bf16),
            jax.ShapeDtypeStruct((N_Y, 2, F_OUT, BLOCK), bf16),
        ),
        in_specs=[vmem()] * 6,
        out_specs=(vmem(), vmem()),
        compiler_params=params,
        name="middle",
    )(scales, parts, scaled, weight_t, bias, cotangent_t)
    group = exchange(send, 3)

    half = jax.ShapeDtypeStruct((N_X, N_Z + 1, F_OUT, BLOCK), bf16)
    keep, away, mixed_t = pl.pallas_call(
        backward_kernel,
        out_shape=(half, half, jax.ShapeDtypeStruct((F_OUT, BLOCK), bf16)),
        in_specs=[anywhere()] * 3 + [vmem()] * 3,
        out_specs=(vmem(), vmem(), anywhere()),
        scratch_shapes=[
            *lists,
            pltpu.VMEM((2 * HALF + 1, F_OUT, BLOCK), f32),
            pltpu.SemaphoreType.DMA((4,)),
        ],
        compiler_params=params,
        name="backward",
    )(tile_row, tile_col, tile_count, group, tile_values, mixed_here)
    recv = swap_cores(away)
    by_core = pl.pallas_call(
        core_sum_kernel,
        out_shape=half,
        in_specs=[vmem()] * 2,
        out_specs=vmem(),
        compiler_params=params,
        name="core_sum",
    )(keep, recv)
    by_x = exchange(by_core, 1)
    by_x = pl.pallas_call(
        x_sum_kernel,
        out_shape=jax.ShapeDtypeStruct((N_Z, 2, F_OUT, BLOCK), bf16),
        in_specs=[vmem()],
        out_specs=vmem(),
        compiler_params=params,
        name="x_sum",
    )(by_x)
    last = exchange(by_x, 0)
    grad_features, grad_weight_t = pl.pallas_call(
        final_kernel,
        out_shape=(
            jax.ShapeDtypeStruct((BLOCK, F_IN), bf16),
            jax.ShapeDtypeStruct((F_OUT, F_IN), f32),
        ),
        in_specs=[vmem()] * 4,
        out_specs=(vmem(), vmem()),
        compiler_params=params,
        name="final",
    )(scales, last, send, weight_t)
    return (mixed_t.T, grad_features, grad_weight_t.T)


def solution(mesh):
    line = Mesh(np.asarray(mesh.devices).reshape(-1), ("d",))
    in_specs = (P("d", None), P("d"), P("d", None, None), P("d"), P("d"), P("d"), P(), P(), P("d", None))
    out_specs = (P("d", None), P("d", None), P())
    return jax.shard_map(shards, mesh=line, in_specs=in_specs, out_specs=out_specs, check_vma=False)
```

```python
import numpy as np

import jax
import jax.numpy as jnp
from jax import lax
from jax.experimental import pallas as pl
from jax.experimental.pallas import tpu as pltpu
from jax.sharding import Mesh, PartitionSpec as P

N_Z, N_X, N_C, N_Y = 8, 4, 2, 8
SIZES = (N_Z, N_X, N_C, N_Y)
BLOCK = 128
F_IN = 128
F_OUT = 64
CHUNK = 48
GROUP = 8
HALF = N_X * N_Z
VMEM_BYTES = 16 * 1024 * 1024
f32 = jnp.float32
bf16 = jnp.bfloat16


def scale_square(scales_ref):
    return jnp.transpose(jnp.broadcast_to(scales_ref[...], (BLOCK, BLOCK)))


def own_core():
    return jnp.bitwise_and(lax.shift_right_logical(lax.axis_index("d"), 3), 1)


def turned(number):
    low, high = jnp.bitwise_and(number, 1), lax.shift_right_logical(number, 2)
    return lax.shift_left(low, 2) + jnp.bitwise_and(number, 2) + high


def place_of(col, core, last):
    owner = lax.shift_right_logical(col, 3)
    z = lax.shift_right_logical(owner, 3)
    x = jnp.bitwise_and(lax.shift_right_logical(owner, 1), 3)
    half = jnp.bitwise_and(owner, 1)
    x = jnp.bitwise_xor(x, half * (N_X - 1))
    x = lax.shift_left(jnp.bitwise_and(x, 1), 1) + lax.shift_right_logical(x, 1)
    z = N_Z - 1 - z if last else turned(jnp.bitwise_xor(jnp.bitwise_xor(z, half), N_Z - 1))
    return jnp.bitwise_xor(half, core) * HALF + x * N_Z + z


def place_in_group(row, core):
    return turned(jnp.bitwise_xor(jnp.bitwise_xor(jnp.bitwise_and(row, N_Y - 1), core), N_Y - 1))


def exchange(blocks, axis, last=False):
    size = SIZES[axis]
    numbers = np.moveaxis(np.arange(np.prod(SIZES)).reshape(SIZES), axis, -1)
    cores = numbers[..., 0].reshape(-1) // N_Y % N_C
    groups = []
    for group, core in zip(numbers.reshape(-1, size), cores):
        if last:
            order = list(range(size))[::-1]
        elif size == 8:
            order = [k ^ 7 ^ int(core) for k in (0, 4, 2, 6, 1, 5, 3, 7)]
        else:
            order = [k ^ (3 * int(core)) for k in (0, 2, 1, 3)]
        groups.append([int(group[k]) for k in order])
    return lax.all_to_all(blocks, "d", 0, 0, axis_index_groups=groups)


def swap_cores(blocks):
    return lax.ppermute(blocks, "d", [(i, i ^ N_Y) for i in range(np.prod(SIZES))])


def start_kernel(scales_ref, features_ref, scaled_ref):
    scaled = (scale_square(scales_ref) * features_ref[...].astype(f32)).astype(bf16)
    scaled_ref[...] = jnp.broadcast_to(scaled[None], scaled_ref.shape)


def slot_copies(rows_ref, cols_ref, count_ref, rows, cols, count, sems):
    pairs = ((rows_ref, rows), (cols_ref, cols), (count_ref, count))
    return [pltpu.make_async_copy(src, dst, sems.at[i]) for i, (src, dst) in enumerate(pairs)]


def forward_kernel(
    rows_any, cols_any, count_any, own_ref, other_ref, values_ref, out_ref,
    rows_ref, cols_ref, count_ref, gathered, acc, sems,
):
    copies = slot_copies(rows_any, cols_any, count_any, rows_ref, cols_ref, count_ref, sems)
    for copy in copies:
        copy.start()
    core = own_core()
    gathered[0:HALF] = own_ref[...]
    gathered[HALF : 2 * HALF] = other_ref[...]
    acc[...] = jnp.zeros_like(acc)
    for copy in copies:
        copy.wait()
    count = count_ref[0]

    def chunk(i, carry):
        for g in range(0, CHUNK, GROUP):
            slots = [i * CHUNK + g + k for k in range(GROUP)]
            products = [
                jnp.dot(values_ref[t], gathered[place_of(cols_ref[t], core, False)], preferred_element_type=f32)
                for t in slots
            ]
            for t, product in zip(slots, products):
                row = jnp.where(t < count, place_in_group(rows_ref[t], core), N_Y)
                acc[row] += product
        return carry

    lax.fori_loop(0, values_ref.shape[0] // CHUNK, chunk, 0)
    out_ref[...] = acc[0:N_Y].astype(bf16)


def middle_kernel(
    scales_ref, parts_ref, scaled_ref, weight_ref, bias_ref, cotangent_ref, mixed_ref, send_ref
):
    total = jnp.sum(parts_ref[...].astype(f32), axis=0) + scaled_ref[0].astype(f32)
    aggregated = (scale_square(scales_ref) * total).astype(bf16)
    preact = (
        lax.dot_general(weight_ref[...], aggregated, (((1,), (1,)), ((), ())), preferred_element_type=f32)
        + bias_ref[...]
    )
    gate = jax.nn.sigmoid(preact)
    mixed_ref[...] = (preact * gate).astype(bf16)
    slope = gate * (1.0 + preact * (1.0 - gate))
    grad_pre = (cotangent_ref[...].astype(f32) * slope).astype(bf16)
    lifted = (scales_ref[...] * grad_pre.astype(f32)).astype(bf16)
    weight_part = jnp.dot(grad_pre, aggregated, preferred_element_type=f32).astype(bf16)
    send_ref[:, 0] = jnp.broadcast_to(lifted[None], (N_Y, F_OUT, BLOCK))
    send_ref[:, 1] = jnp.broadcast_to(weight_part[None], (N_Y, F_OUT, F_IN))


def backward_kernel(
    rows_any, cols_any, count_any, group_ref, values_ref, mixed_ref, keep_ref, send_ref, mixed_any,
    rows_ref, cols_ref, count_ref, acc, sems,
):
    copies = slot_copies(rows_any, cols_any, count_any, rows_ref, cols_ref, count_ref, sems)
    mixed_copy = pltpu.make_async_copy(mixed_ref, mixed_any, sems.at[3])
    for copy in copies:
        copy.start()
    mixed_copy.start()
    core = own_core()
    acc[...] = jnp.zeros_like(acc)
    for copy in copies:
        copy.wait()
    count = count_ref[0]

    def chunk(i, carry):
        for g in range(0, CHUNK, GROUP):
            slots = [i * CHUNK + g + k for k in range(GROUP)]
            products = [
                jnp.dot(
                    group_ref[place_in_group(rows_ref[t], core), 0],
                    values_ref[t],
                    preferred_element_type=f32,
                )
                for t in slots
            ]
            for t, product in zip(slots, products):
                place = jnp.where(t < count, place_of(cols_ref[t], core, True), 2 * HALF)
                acc[place] += product
        return carry

    lax.fori_loop(0, values_ref.shape[0] // CHUNK, chunk, 0)
    weight_part = jnp.sum(group_ref[:, 1].astype(f32), axis=0).astype(bf16)
    for x in range(N_X):
        keep_ref[x, 0:N_Z] = acc[x * N_Z : (x + 1) * N_Z].astype(bf16)
        send_ref[x, 0:N_Z] = acc[HALF + x * N_Z : HALF + (x + 1) * N_Z].astype(bf16)
        keep_ref[x, N_Z] = weight_part
        send_ref[x, N_Z] = weight_part
    mixed_copy.wait()


def core_sum_kernel(keep_ref, recv_ref, out_ref):
    out_ref[...] = (keep_ref[...].astype(f32) + recv_ref[...].astype(f32)).astype(bf16)


def x_sum_kernel(recv_ref, out_ref):
    total = jnp.sum(recv_ref[...].astype(f32), axis=0).astype(bf16)
    out_ref[:, 0] = total[0:N_Z]
    out_ref[:, 1] = jnp.broadcast_to(total[N_Z][None], (N_Z, F_OUT, F_IN))


def final_kernel(scales_ref, recv_ref, sent_ref, weight_ref, grad_features_ref, grad_weight_ref):
    total = jnp.sum(recv_ref[...].astype(f32), axis=0)
    grad_scaled = scales_ref[...] * (total[0] + sent_ref[0, 0].astype(f32))
    turned = jnp.transpose(grad_scaled).astype(bf16)
    grad_features_ref[...] = jnp.dot(turned, weight_ref[...], preferred_element_type=f32).astype(bf16)
    node_total = BLOCK * N_Z * N_X * N_C * N_Y
    grad_weight_ref[...] = total[1] * (1.0 / np.sqrt(node_total))


def vmem():
    return pl.BlockSpec(memory_space=pltpu.VMEM)


def anywhere():
    return pl.BlockSpec(memory_space=pl.ANY)


def shards(
    features, degrees, tile_values, tile_row, tile_col, tile_count, weight, out_bias, cotangent
):
    slots = tile_values.shape[0]
    scales = lax.rsqrt(degrees.astype(f32) + 1.0).reshape(1, BLOCK)
    weight_t = weight.T
    cotangent_t = cotangent.T
    bias = jnp.broadcast_to(out_bias.astype(f32)[:, None], (F_OUT, BLOCK))
    lists = [pltpu.SMEM((slots,), jnp.int32), pltpu.SMEM((slots,), jnp.int32), pltpu.SMEM((1,), jnp.int32)]
    params = pltpu.CompilerParams(vmem_limit_bytes=VMEM_BYTES)

    scaled = pl.pallas_call(
        start_kernel,
        out_shape=jax.ShapeDtypeStruct((N_Z, BLOCK, F_IN), bf16),
        in_specs=[vmem()] * 2,
        out_specs=vmem(),
        compiler_params=params,
        name="start",
    )(scales, features)
    by_z = exchange(scaled, 0)
    by_xz = exchange(jnp.broadcast_to(by_z[None], (N_X,) + by_z.shape), 1)
    own = by_xz.reshape(HALF, BLOCK, F_IN)
    other = swap_cores(own)

    parts = pl.pallas_call(
        forward_kernel,
        out_shape=jax.ShapeDtypeStruct((N_Y, BLOCK, F_IN), bf16),
        in_specs=[anywhere()] * 3 + [vmem()] * 3,
        out_specs=vmem(),
        scratch_shapes=[
            *lists,
            pltpu.VMEM((2 * HALF, BLOCK, F_IN), bf16),
            pltpu.VMEM((N_Y + 1, BLOCK, F_IN), f32),
            pltpu.SemaphoreType.DMA((3,)),
        ],
        compiler_params=params,
        name="forward",
    )(tile_row, tile_col, tile_count, own, other, tile_values)
    parts = exchange(parts, 3)

    mixed_here, send = pl.pallas_call(
        middle_kernel,
        out_shape=(
            jax.ShapeDtypeStruct((F_OUT, BLOCK), bf16),
            jax.ShapeDtypeStruct((N_Y, 2, F_OUT, BLOCK), bf16),
        ),
        in_specs=[vmem()] * 6,
        out_specs=(vmem(), vmem()),
        compiler_params=params,
        name="middle",
    )(scales, parts, scaled, weight_t, bias, cotangent_t)
    group = exchange(send, 3)

    half = jax.ShapeDtypeStruct((N_X, N_Z + 1, F_OUT, BLOCK), bf16)
    keep, away, mixed_t = pl.pallas_call(
        backward_kernel,
        out_shape=(half, half, jax.ShapeDtypeStruct((F_OUT, BLOCK), bf16)),
        in_specs=[anywhere()] * 3 + [vmem()] * 3,
        out_specs=(vmem(), vmem(), anywhere()),
        scratch_shapes=[
            *lists,
            pltpu.VMEM((2 * HALF + 1, F_OUT, BLOCK), f32),
            pltpu.SemaphoreType.DMA((4,)),
        ],
        compiler_params=params,
        name="backward",
    )(tile_row, tile_col, tile_count, group, tile_values, mixed_here)
    recv = swap_cores(away)
    by_core = pl.pallas_call(
        core_sum_kernel,
        out_shape=half,
        in_specs=[vmem()] * 2,
        out_specs=vmem(),
        compiler_params=params,
        name="core_sum",
    )(keep, recv)
    by_x = exchange(by_core, 1)
    by_x = pl.pallas_call(
        x_sum_kernel,
        out_shape=jax.ShapeDtypeStruct((N_Z, 2, F_OUT, BLOCK), bf16),
        in_specs=[vmem()],
        out_specs=vmem(),
        compiler_params=params,
        name="x_sum",
    )(by_x)
    last = exchange(by_x, 0, last=True)
    grad_features, grad_weight_t = pl.pallas_call(
        final_kernel,
        out_shape=(
            jax.ShapeDtypeStruct((BLOCK, F_IN), bf16),
            jax.ShapeDtypeStruct((F_OUT, F_IN), f32),
        ),
        in_specs=[vmem()] * 4,
        out_specs=(vmem(), vmem()),
        compiler_params=params,
        name="final",
    )(scales, last, send, weight_t)
    return (mixed_t.T, grad_features, grad_weight_t.T)


def solution(mesh):
    line = Mesh(np.asarray(mesh.devices).reshape(-1), ("d",))
    in_specs = (P("d", None), P("d"), P("d", None, None), P("d"), P("d"), P("d"), P(), P(), P("d", None))
    out_specs = (P("d", None), P("d", None), P())
    return jax.shard_map(shards, mesh=line, in_specs=in_specs, out_specs=out_specs, check_vma=False)
```

```python
import numpy as np

import jax
import jax.numpy as jnp
from jax import lax
from jax.experimental import pallas as pl
from jax.experimental.pallas import tpu as pltpu
from jax.sharding import Mesh, PartitionSpec as P

N_Z, N_X, N_C, N_Y = 8, 4, 2, 8
SIZES = (N_Z, N_X, N_C, N_Y)
BLOCK = 128
F_IN = 128
F_OUT = 64
CHUNK = 48
GROUP = 8
HALF = N_X * N_Z
VMEM_BYTES = 16 * 1024 * 1024
f32 = jnp.float32
bf16 = jnp.bfloat16


def scale_square(scales_ref):
    return jnp.transpose(jnp.broadcast_to(scales_ref[...], (BLOCK, BLOCK)))


def own_core():
    return jnp.bitwise_and(lax.shift_right_logical(lax.axis_index("d"), 3), 1)


def turned(number):
    low, high = jnp.bitwise_and(number, 1), lax.shift_right_logical(number, 2)
    return lax.shift_left(low, 2) + jnp.bitwise_and(number, 2) + high


def place_of(col, core):
    owner = lax.shift_right_logical(col, 3)
    z = lax.shift_right_logical(owner, 3)
    half = jnp.bitwise_and(owner, 1)
    x = jnp.bitwise_xor(jnp.bitwise_and(lax.shift_right_logical(owner, 1), 3), 2 * half)
    x = jnp.bitwise_xor(x, lax.shift_right_logical(x, 1))
    z = turned(jnp.bitwise_xor(jnp.bitwise_xor(z, half), N_Z - 1))
    return jnp.bitwise_xor(half, core) * HALF + x * N_Z + z


def place_in_group(row, core):
    return turned(jnp.bitwise_xor(jnp.bitwise_xor(jnp.bitwise_and(row, N_Y - 1), core), N_Y - 1))


def exchange(blocks, axis):
    size = SIZES[axis]
    numbers = np.moveaxis(np.arange(np.prod(SIZES)).reshape(SIZES), axis, -1)
    cores = numbers[..., 0].reshape(-1) // N_Y % N_C
    groups = []
    for group, core in zip(numbers.reshape(-1, size), cores):
        if size == 8:
            order = [k ^ 7 ^ int(core) for k in (0, 4, 2, 6, 1, 5, 3, 7)]
        else:
            order = [k ^ (2 * int(core)) for k in (0, 1, 3, 2)]
        groups.append([int(group[k]) for k in order])
    return lax.all_to_all(blocks, "d", 0, 0, axis_index_groups=groups)


def swap_cores(blocks):
    return lax.ppermute(blocks, "d", [(i, i ^ N_Y) for i in range(np.prod(SIZES))])


def start_kernel(scales_ref, features_ref, scaled_ref):
    scaled = (scale_square(scales_ref) * features_ref[...].astype(f32)).astype(bf16)
    scaled_ref[...] = jnp.broadcast_to(scaled[None], scaled_ref.shape)


def slot_copies(rows_ref, cols_ref, count_ref, rows, cols, count, sems):
    pairs = ((rows_ref, rows), (cols_ref, cols), (count_ref, count))
    return [pltpu.make_async_copy(src, dst, sems.at[i]) for i, (src, dst) in enumerate(pairs)]


def forward_kernel(
    rows_any, cols_any, count_any, own_ref, other_ref, values_ref, out_ref,
    rows_ref, cols_ref, count_ref, gathered, acc, sems,
):
    copies = slot_copies(rows_any, cols_any, count_any, rows_ref, cols_ref, count_ref, sems)
    for copy in copies:
        copy.start()
    core = own_core()
    gathered[0:HALF] = own_ref[...]
    gathered[HALF : 2 * HALF] = other_ref[...]
    acc[...] = jnp.zeros_like(acc)
    for copy in copies:
        copy.wait()
    count = count_ref[0]

    def chunk(i, carry):
        for g in range(0, CHUNK, GROUP):
            slots = [i * CHUNK + g + k for k in range(GROUP)]
            products = [
                jnp.dot(values_ref[t], gathered[place_of(cols_ref[t], core)], preferred_element_type=f32)
                for t in slots
            ]
            for t, product in zip(slots, products):
                row = jnp.where(t < count, place_in_group(rows_ref[t], core), N_Y)
                acc[row] += product
        return carry

    lax.fori_loop(0, values_ref.shape[0] // CHUNK, chunk, 0)
    out_ref[...] = acc[0:N_Y].astype(bf16)


def middle_kernel(
    scales_ref, parts_ref, scaled_ref, weight_ref, bias_ref, cotangent_ref, mixed_ref, send_ref
):
    total = jnp.sum(parts_ref[...].astype(f32), axis=0) + scaled_ref[0].astype(f32)
    aggregated = (scale_square(scales_ref) * total).astype(bf16)
    preact = (
        lax.dot_general(weight_ref[...], aggregated, (((1,), (1,)), ((), ())), preferred_element_type=f32)
        + bias_ref[...]
    )
    gate = jax.nn.sigmoid(preact)
    mixed_ref[...] = (preact * gate).astype(bf16)
    slope = gate * (1.0 + preact * (1.0 - gate))
    grad_pre = (cotangent_ref[...].astype(f32) * slope).astype(bf16)
    lifted = (scales_ref[...] * grad_pre.astype(f32)).astype(bf16)
    weight_part = jnp.dot(grad_pre, aggregated, preferred_element_type=f32).astype(bf16)
    send_ref[:, 0] = jnp.broadcast_to(lifted[None], (N_Y, F_OUT, BLOCK))
    send_ref[:, 1] = jnp.broadcast_to(weight_part[None], (N_Y, F_OUT, F_IN))


def backward_kernel(
    rows_any, cols_any, count_any, group_ref, values_ref, mixed_ref, keep_ref, send_ref, mixed_any,
    rows_ref, cols_ref, count_ref, acc, sems,
):
    copies = slot_copies(rows_any, cols_any, count_any, rows_ref, cols_ref, count_ref, sems)
    mixed_copy = pltpu.make_async_copy(mixed_ref, mixed_any, sems.at[3])
    for copy in copies:
        copy.start()
    mixed_copy.start()
    core = own_core()
    acc[...] = jnp.zeros_like(acc)
    for copy in copies:
        copy.wait()
    count = count_ref[0]

    def chunk(i, carry):
        for g in range(0, CHUNK, GROUP):
            slots = [i * CHUNK + g + k for k in range(GROUP)]
            products = [
                jnp.dot(
                    group_ref[place_in_group(rows_ref[t], core), 0],
                    values_ref[t],
                    preferred_element_type=f32,
                )
                for t in slots
            ]
            for t, product in zip(slots, products):
                place = jnp.where(t < count, place_of(cols_ref[t], core), 2 * HALF)
                acc[place] += product
        return carry

    lax.fori_loop(0, values_ref.shape[0] // CHUNK, chunk, 0)
    weight_part = jnp.sum(group_ref[:, 1].astype(f32), axis=0).astype(bf16)
    for x in range(N_X):
        keep_ref[x, 0:N_Z] = acc[x * N_Z : (x + 1) * N_Z].astype(bf16)
        send_ref[x, 0:N_Z] = acc[HALF + x * N_Z : HALF + (x + 1) * N_Z].astype(bf16)
        keep_ref[x, N_Z] = weight_part
        send_ref[x, N_Z] = weight_part
    mixed_copy.wait()


def core_sum_kernel(keep_ref, recv_ref, out_ref):
    out_ref[...] = (keep_ref[...].astype(f32) + recv_ref[...].astype(f32)).astype(bf16)


def x_sum_kernel(recv_ref, out_ref):
    total = jnp.sum(recv_ref[...].astype(f32), axis=0).astype(bf16)
    out_ref[:, 0] = total[0:N_Z]
    out_ref[:, 1] = jnp.broadcast_to(total[N_Z][None], (N_Z, F_OUT, F_IN))


def final_kernel(scales_ref, recv_ref, sent_ref, weight_ref, grad_features_ref, grad_weight_ref):
    total = jnp.sum(recv_ref[...].astype(f32), axis=0)
    grad_scaled = scales_ref[...] * (total[0] + sent_ref[0, 0].astype(f32))
    turned = jnp.transpose(grad_scaled).astype(bf16)
    grad_features_ref[...] = jnp.dot(turned, weight_ref[...], preferred_element_type=f32).astype(bf16)
    node_total = BLOCK * N_Z * N_X * N_C * N_Y
    grad_weight_ref[...] = total[1] * (1.0 / np.sqrt(node_total))


def vmem():
    return pl.BlockSpec(memory_space=pltpu.VMEM)


def anywhere():
    return pl.BlockSpec(memory_space=pl.ANY)


def shards(
    features, degrees, tile_values, tile_row, tile_col, tile_count, weight, out_bias, cotangent
):
    slots = tile_values.shape[0]
    scales = lax.rsqrt(degrees.astype(f32) + 1.0).reshape(1, BLOCK)
    weight_t = weight.T
    cotangent_t = cotangent.T
    bias = jnp.broadcast_to(out_bias.astype(f32)[:, None], (F_OUT, BLOCK))
    lists = [pltpu.SMEM((slots,), jnp.int32), pltpu.SMEM((slots,), jnp.int32), pltpu.SMEM((1,), jnp.int32)]
    params = pltpu.CompilerParams(vmem_limit_bytes=VMEM_BYTES)

    scaled = pl.pallas_call(
        start_kernel,
        out_shape=jax.ShapeDtypeStruct((N_Z, BLOCK, F_IN), bf16),
        in_specs=[vmem()] * 2,
        out_specs=vmem(),
        compiler_params=params,
        name="start",
    )(scales, features)
    by_z = exchange(scaled, 0)
    by_xz = exchange(jnp.broadcast_to(by_z[None], (N_X,) + by_z.shape), 1)
    own = by_xz.reshape(HALF, BLOCK, F_IN)
    other = swap_cores(own)

    parts = pl.pallas_call(
        forward_kernel,
        out_shape=jax.ShapeDtypeStruct((N_Y, BLOCK, F_IN), bf16),
        in_specs=[anywhere()] * 3 + [vmem()] * 3,
        out_specs=vmem(),
        scratch_shapes=[
            *lists,
            pltpu.VMEM((2 * HALF, BLOCK, F_IN), bf16),
            pltpu.VMEM((N_Y + 1, BLOCK, F_IN), f32),
            pltpu.SemaphoreType.DMA((3,)),
        ],
        compiler_params=params,
        name="forward",
    )(tile_row, tile_col, tile_count, own, other, tile_values)
    parts = exchange(parts, 3)

    mixed_here, send = pl.pallas_call(
        middle_kernel,
        out_shape=(
            jax.ShapeDtypeStruct((F_OUT, BLOCK), bf16),
            jax.ShapeDtypeStruct((N_Y, 2, F_OUT, BLOCK), bf16),
        ),
        in_specs=[vmem()] * 6,
        out_specs=(vmem(), vmem()),
        compiler_params=params,
        name="middle",
    )(scales, parts, scaled, weight_t, bias, cotangent_t)
    group = exchange(send, 3)

    half = jax.ShapeDtypeStruct((N_X, N_Z + 1, F_OUT, BLOCK), bf16)
    keep, away, mixed_t = pl.pallas_call(
        backward_kernel,
        out_shape=(half, half, jax.ShapeDtypeStruct((F_OUT, BLOCK), bf16)),
        in_specs=[anywhere()] * 3 + [vmem()] * 3,
        out_specs=(vmem(), vmem(), anywhere()),
        scratch_shapes=[
            *lists,
            pltpu.VMEM((2 * HALF + 1, F_OUT, BLOCK), f32),
            pltpu.SemaphoreType.DMA((4,)),
        ],
        compiler_params=params,
        name="backward",
    )(tile_row, tile_col, tile_count, group, tile_values, mixed_here)
    recv = swap_cores(away)
    by_core = pl.pallas_call(
        core_sum_kernel,
        out_shape=half,
        in_specs=[vmem()] * 2,
        out_specs=vmem(),
        compiler_params=params,
        name="core_sum",
    )(keep, recv)
    by_x = exchange(by_core, 1)
    by_x = pl.pallas_call(
        x_sum_kernel,
        out_shape=jax.ShapeDtypeStruct((N_Z, 2, F_OUT, BLOCK), bf16),
        in_specs=[vmem()],
        out_specs=vmem(),
        compiler_params=params,
        name="x_sum",
    )(by_x)
    last = exchange(by_x, 0)
    grad_features, grad_weight_t = pl.pallas_call(
        final_kernel,
        out_shape=(
            jax.ShapeDtypeStruct((BLOCK, F_IN), bf16),
            jax.ShapeDtypeStruct((F_OUT, F_IN), f32),
        ),
        in_specs=[vmem()] * 4,
        out_specs=(vmem(), vmem()),
        compiler_params=params,
        name="final",
    )(scales, last, send, weight_t)
    return (mixed_t.T, grad_features, grad_weight_t.T)


def solution(mesh):
    line = Mesh(np.asarray(mesh.devices).reshape(-1), ("d",))
    in_specs = (P("d", None), P("d"), P("d", None, None), P("d"), P("d"), P("d"), P(), P(), P("d", None))
    out_specs = (P("d", None), P("d", None), P())
    return jax.shard_map(shards, mesh=line, in_specs=in_specs, out_specs=out_specs, check_vma=False)
```

```python
import numpy as np

import jax
import jax.numpy as jnp
from jax import lax
from jax.experimental import pallas as pl
from jax.experimental.pallas import tpu as pltpu
from jax.sharding import Mesh, PartitionSpec as P

N_Z, N_X, N_C, N_Y = 8, 4, 2, 8
SIZES = (N_Z, N_X, N_C, N_Y)
BLOCK = 128
F_IN = 128
F_OUT = 64
CHUNK = 48
GROUP = 8
HALF = N_X * N_Z
VMEM_BYTES = 16 * 1024 * 1024
f32 = jnp.float32
bf16 = jnp.bfloat16


def scale_square(scales_ref):
    return jnp.transpose(jnp.broadcast_to(scales_ref[...], (BLOCK, BLOCK)))


def own_core():
    return jnp.bitwise_and(lax.shift_right_logical(lax.axis_index("d"), 3), 1)


def turned(number):
    low, high = jnp.bitwise_and(number, 1), lax.shift_right_logical(number, 2)
    return lax.shift_left(low, 2) + jnp.bitwise_and(number, 2) + high


def place_of(col, core):
    owner = lax.shift_right_logical(col, 3)
    z = lax.shift_right_logical(owner, 3)
    half = jnp.bitwise_and(owner, 1)
    x = jnp.bitwise_xor(jnp.bitwise_and(lax.shift_right_logical(owner, 1), 3), 3 * half)
    x = lax.shift_left(jnp.bitwise_and(x, 1), 1) + lax.shift_right_logical(x, 1)
    z = turned(jnp.bitwise_xor(jnp.bitwise_xor(z, half), N_Z - 1))
    return jnp.bitwise_xor(half, core) * HALF + x * N_Z + z


def place_in_group(row, core):
    return turned(jnp.bitwise_xor(jnp.bitwise_xor(jnp.bitwise_and(row, N_Y - 1), core), N_Y - 1))


def exchange(blocks, axis):
    size = SIZES[axis]
    numbers = np.moveaxis(np.arange(np.prod(SIZES)).reshape(SIZES), axis, -1)
    cores = numbers[..., 0].reshape(-1) // N_Y % N_C
    groups = []
    for group, core in zip(numbers.reshape(-1, size), cores):
        if size == 8:
            order = [k ^ 7 ^ int(core) for k in (0, 4, 2, 6, 1, 5, 3, 7)]
        else:
            order = [k ^ (3 * int(core)) for k in (0, 2, 1, 3)]
        groups.append([int(group[k]) for k in order])
    return lax.all_to_all(blocks, "d", 0, 0, axis_index_groups=groups)


def swap_cores(blocks):
    return lax.ppermute(blocks, "d", [(i, i ^ N_Y) for i in range(np.prod(SIZES))])


def start_kernel(scales_ref, features_ref, scaled_ref):
    scaled = (scale_square(scales_ref) * features_ref[...].astype(f32)).astype(bf16)
    scaled_ref[...] = jnp.broadcast_to(scaled[None], scaled_ref.shape)


def slot_copies(rows_ref, cols_ref, count_ref, rows, cols, count, sems):
    pairs = ((rows_ref, rows), (cols_ref, cols), (count_ref, count))
    return [pltpu.make_async_copy(src, dst, sems.at[i]) for i, (src, dst) in enumerate(pairs)]


def forward_kernel(
    rows_any, cols_any, count_any, own_ref, other_ref, values_ref, out_ref,
    rows_ref, cols_ref, count_ref, gathered, acc, sems,
):
    copies = slot_copies(rows_any, cols_any, count_any, rows_ref, cols_ref, count_ref, sems)
    for copy in copies:
        copy.start()
    core = own_core()
    gathered[0:HALF] = own_ref[...]
    gathered[HALF : 2 * HALF] = other_ref[...]
    acc[...] = jnp.zeros_like(acc)
    for copy in copies:
        copy.wait()
    count = count_ref[0]

    def chunk(i, carry):
        for g in range(0, CHUNK, GROUP):
            slots = [i * CHUNK + g + k for k in range(GROUP)]
            products = [
                jnp.dot(values_ref[t], gathered[place_of(cols_ref[t], core)], preferred_element_type=f32)
                for t in slots
            ]
            for t, product in zip(slots, products):
                row = jnp.where(t < count, place_in_group(rows_ref[t], core), N_Y)
                acc[row] += product
        return carry

    lax.fori_loop(0, values_ref.shape[0] // CHUNK, chunk, 0)
    out_ref[...] = acc[0:N_Y].astype(bf16)


def middle_kernel(
    scales_ref, parts_ref, scaled_ref, weight_ref, bias_ref, cotangent_ref, mixed_ref, send_ref
):
    total = jnp.sum(parts_ref[...].astype(f32), axis=0) + scaled_ref[0].astype(f32)
    aggregated = (scale_square(scales_ref) * total).astype(bf16)
    preact = (
        lax.dot_general(weight_ref[...], aggregated, (((1,), (1,)), ((), ())), preferred_element_type=f32)
        + bias_ref[...]
    )
    gate = jax.nn.sigmoid(preact)
    mixed_ref[...] = (preact * gate).astype(bf16)
    slope = gate * (1.0 + preact * (1.0 - gate))
    grad_pre = (cotangent_ref[...].astype(f32) * slope).astype(bf16)
    lifted = (scales_ref[...] * grad_pre.astype(f32)).astype(bf16)
    weight_part = jnp.dot(grad_pre, aggregated, preferred_element_type=f32).astype(bf16)
    send_ref[:, 0] = jnp.broadcast_to(lifted[None], (N_Y, F_OUT, BLOCK))
    send_ref[:, 1] = jnp.broadcast_to(weight_part[None], (N_Y, F_OUT, F_IN))


def backward_kernel(
    rows_any, cols_any, count_any, group_ref, values_ref, mixed_ref, keep_ref, send_ref, mixed_any,
    rows_ref, cols_ref, count_ref, acc, sems,
):
    copies = slot_copies(rows_any, cols_any, count_any, rows_ref, cols_ref, count_ref, sems)
    mixed_copy = pltpu.make_async_copy(mixed_ref, mixed_any, sems.at[3])
    for copy in copies:
        copy.start()
    mixed_copy.start()
    core = own_core()
    acc[...] = jnp.zeros_like(acc)
    for copy in copies:
        copy.wait()
    count = count_ref[0]

    def chunk(i, carry):
        for g in range(0, CHUNK, GROUP):
            slots = [i * CHUNK + g + k for k in range(GROUP)]
            products = [
                jnp.dot(
                    group_ref[place_in_group(rows_ref[t], core), 0],
                    values_ref[t],
                    preferred_element_type=f32,
                )
                for t in slots
            ]
            for t, product in zip(slots, products):
                place = jnp.where(t < count, place_of(cols_ref[t], core), 2 * HALF)
                acc[place] += product
        return carry

    lax.fori_loop(0, values_ref.shape[0] // CHUNK, chunk, 0)
    weight_part = jnp.sum(group_ref[:, 1].astype(f32), axis=0).astype(bf16)
    for x in range(N_X):
        keep_ref[x, 0:N_Z] = acc[x * N_Z : (x + 1) * N_Z].astype(bf16)
        send_ref[x, 0:N_Z] = acc[HALF + x * N_Z : HALF + (x + 1) * N_Z].astype(bf16)
        keep_ref[x, N_Z] = weight_part
        send_ref[x, N_Z] = weight_part
    mixed_copy.wait()


def core_sum_kernel(keep_ref, recv_ref, out_ref):
    out_ref[...] = (keep_ref[...].astype(f32) + recv_ref[...].astype(f32)).astype(bf16)


def x_sum_kernel(recv_ref, out_ref):
    total = jnp.sum(recv_ref[...].astype(f32), axis=0).astype(bf16)
    out_ref[:, 0] = total[0:N_Z]
    out_ref[:, 1] = jnp.broadcast_to(total[N_Z][None], (N_Z, F_OUT, F_IN))


def final_kernel(scales_ref, recv_ref, sent_ref, weight_ref, grad_features_ref, grad_weight_ref):
    total = jnp.sum(recv_ref[...].astype(f32), axis=0)
    grad_scaled = scales_ref[...] * (total[0] + sent_ref[0, 0].astype(f32))
    turned = jnp.transpose(grad_scaled).astype(bf16)
    grad_features_ref[...] = jnp.dot(turned, weight_ref[...], preferred_element_type=f32).astype(bf16)
    node_total = BLOCK * N_Z * N_X * N_C * N_Y
    grad_weight_ref[...] = total[1] * (1.0 / np.sqrt(node_total))


def vmem():
    return pl.BlockSpec(memory_space=pltpu.VMEM)


def anywhere():
    return pl.BlockSpec(memory_space=pl.ANY)


def shards(
    features, degrees, tile_values, tile_row, tile_col, tile_count, weight, out_bias, cotangent
):
    slots = tile_values.shape[0]
    scales = lax.rsqrt(degrees.astype(f32) + 1.0).reshape(1, BLOCK)
    weight_t = weight.T
    cotangent_t = cotangent.T
    bias = jnp.broadcast_to(out_bias.astype(f32)[:, None], (F_OUT, BLOCK))
    lists = [pltpu.SMEM((slots,), jnp.int32), pltpu.SMEM((slots,), jnp.int32), pltpu.SMEM((1,), jnp.int32)]
    params = pltpu.CompilerParams(vmem_limit_bytes=VMEM_BYTES)

    scaled = pl.pallas_call(
        start_kernel,
        out_shape=jax.ShapeDtypeStruct((N_Z, BLOCK, F_IN), bf16),
        in_specs=[vmem()] * 2,
        out_specs=vmem(),
        compiler_params=params,
        name="start",
    )(scales, features)
    by_z = exchange(scaled, 0)
    by_xz = exchange(jnp.broadcast_to(by_z[None], (N_X,) + by_z.shape), 1)
    own = by_xz.reshape(HALF, BLOCK, F_IN)
    other = swap_cores(own)

    parts = pl.pallas_call(
        forward_kernel,
        out_shape=jax.ShapeDtypeStruct((N_Y, BLOCK, F_IN), bf16),
        in_specs=[anywhere()] * 3 + [vmem()] * 3,
        out_specs=vmem(),
        scratch_shapes=[
            *lists,
            pltpu.VMEM((2 * HALF, BLOCK, F_IN), bf16),
            pltpu.VMEM((N_Y + 1, BLOCK, F_IN), f32),
            pltpu.SemaphoreType.DMA((3,)),
        ],
        compiler_params=params,
        name="forward",
    )(tile_row, tile_col, tile_count, own, other, tile_values)
    parts = exchange(parts, 3)

    mixed_here, send = pl.pallas_call(
        middle_kernel,
        out_shape=(
            jax.ShapeDtypeStruct((F_OUT, BLOCK), bf16),
            jax.ShapeDtypeStruct((N_Y, 2, F_OUT, BLOCK), bf16),
        ),
        in_specs=[vmem()] * 6,
        out_specs=(vmem(), vmem()),
        compiler_params=params,
        name="middle",
    )(scales, parts, scaled, weight_t, bias, cotangent_t)
    group = exchange(send, 3)

    half = jax.ShapeDtypeStruct((N_X, N_Z + 1, F_OUT, BLOCK), bf16)
    keep, away, mixed_t = pl.pallas_call(
        backward_kernel,
        out_shape=(half, half, jax.ShapeDtypeStruct((F_OUT, BLOCK), bf16)),
        in_specs=[anywhere()] * 3 + [vmem()] * 3,
        out_specs=(vmem(), vmem(), anywhere()),
        scratch_shapes=[
            *lists,
            pltpu.VMEM((2 * HALF + 1, F_OUT, BLOCK), f32),
            pltpu.SemaphoreType.DMA((4,)),
        ],
        compiler_params=params,
        name="backward",
    )(tile_row, tile_col, tile_count, group, tile_values, mixed_here)
    recv = swap_cores(away)
    by_core = pl.pallas_call(
        core_sum_kernel,
        out_shape=half,
        in_specs=[vmem()] * 2,
        out_specs=vmem(),
        compiler_params=params,
        name="core_sum",
    )(keep, recv)
    by_x = exchange(by_core, 1)
    by_x = pl.pallas_call(
        x_sum_kernel,
        out_shape=jax.ShapeDtypeStruct((N_Z, 2, F_OUT, BLOCK), bf16),
        in_specs=[vmem()],
        out_specs=vmem(),
        compiler_params=params,
        name="x_sum",
    )(by_x)
    last = exchange(by_x, 0)
    grad_features, grad_weight_t = pl.pallas_call(
        final_kernel,
        out_shape=(
            jax.ShapeDtypeStruct((BLOCK, F_IN), bf16),
            jax.ShapeDtypeStruct((F_OUT, F_IN), f32),
        ),
        in_specs=[vmem()] * 4,
        out_specs=(vmem(), vmem()),
        compiler_params=params,
        name="final",
    )(scales, last, send, weight_t)
    return (mixed_t.T, grad_features, grad_weight_t.T)


def solution(mesh):
    line = Mesh(np.asarray(mesh.devices).reshape(-1), ("d",))
    in_specs = (P("d", None), P("d"), P("d", None, None), P("d"), P("d"), P("d"), P(), P(), P("d", None))
    out_specs = (P("d", None), P("d", None), P())
    return jax.shard_map(shards, mesh=line, in_specs=in_specs, out_specs=out_specs, check_vma=False)
```

```python
import numpy as np

import jax
import jax.numpy as jnp
from jax import lax
from jax.experimental import pallas as pl
from jax.experimental.pallas import tpu as pltpu
from jax.sharding import Mesh, PartitionSpec as P

N_Z, N_X, N_C, N_Y = 8, 4, 2, 8
SIZES = (N_Z, N_X, N_C, N_Y)
BLOCK = 128
F_IN = 128
F_OUT = 64
CHUNK = 48
GROUP = 8
HALF = N_X * N_Z
VMEM_BYTES = 16 * 1024 * 1024
f32 = jnp.float32
bf16 = jnp.bfloat16


def scale_square(scales_ref):
    return jnp.transpose(jnp.broadcast_to(scales_ref[...], (BLOCK, BLOCK)))


def own_core():
    return jnp.bitwise_and(lax.shift_right_logical(lax.axis_index("d"), 3), 1)


def turned(number):
    low, high = jnp.bitwise_and(number, 1), lax.shift_right_logical(number, 2)
    return lax.shift_left(low, 2) + jnp.bitwise_and(number, 2) + high


def place_of(col, core):
    owner = lax.shift_right_logical(col, 3)
    z = lax.shift_right_logical(owner, 3)
    half = jnp.bitwise_and(owner, 1)
    x = jnp.bitwise_xor(jnp.bitwise_and(lax.shift_right_logical(owner, 1), 3), 2 * half)
    x = jnp.bitwise_xor(x, lax.shift_right_logical(x, 1))
    z = turned(jnp.bitwise_xor(jnp.bitwise_xor(z, half), N_Z - 1))
    return jnp.bitwise_xor(half, core) * HALF + x * N_Z + z


def place_in_group(row, core):
    return turned(jnp.bitwise_xor(jnp.bitwise_xor(jnp.bitwise_and(row, N_Y - 1), core), N_Y - 1))


def exchange(blocks, axis):
    size = SIZES[axis]
    numbers = np.moveaxis(np.arange(np.prod(SIZES)).reshape(SIZES), axis, -1)
    cores = numbers[..., 0].reshape(-1) // N_Y % N_C
    groups = []
    for group, core in zip(numbers.reshape(-1, size), cores):
        if size == 8:
            order = [k ^ 7 ^ int(core) for k in (0, 4, 2, 6, 1, 5, 3, 7)]
        else:
            order = [k ^ (2 * int(core)) for k in (0, 1, 3, 2)]
        groups.append([int(group[k]) for k in order])
    return lax.all_to_all(blocks, "d", 0, 0, axis_index_groups=groups)


def swap_cores(blocks):
    return lax.ppermute(blocks, "d", [(i, i ^ N_Y) for i in range(np.prod(SIZES))])


def list_places(rows_ref, cols_ref, count_ref, core, lists_ref):
    slots = rows_ref.shape[0]
    count = count_ref[0]

    def slot(t, carry):
        live = t < count
        place = place_of(cols_ref[t], core)
        row = place_in_group(rows_ref[t], core)
        lists_ref[t] = place
        lists_ref[slots + t] = row
        lists_ref[2 * slots + t] = jnp.where(live, row, N_Y)
        lists_ref[3 * slots + t] = jnp.where(live, place, 2 * HALF)
        return carry

    lax.fori_loop(0, slots, slot, 0)


def start_kernel(scales_ref, features_ref, scaled_ref):
    scaled = (scale_square(scales_ref) * features_ref[...].astype(f32)).astype(bf16)
    scaled_ref[...] = jnp.broadcast_to(scaled[None], scaled_ref.shape)


def lists_kernel(rows_any, cols_any, count_any, after_any, lists_ref, rows_ref, cols_ref, count_ref, sems):
    del after_any
    copies = slot_copies(rows_any, cols_any, count_any, rows_ref, cols_ref, count_ref, sems)
    for copy in copies:
        copy.start()
    for copy in copies:
        copy.wait()
    list_places(rows_ref, cols_ref, count_ref, own_core(), lists_ref)


def slot_copies(rows_ref, cols_ref, count_ref, rows, cols, count, sems):
    pairs = ((rows_ref, rows), (cols_ref, cols), (count_ref, count))
    return [pltpu.make_async_copy(src, dst, sems.at[i]) for i, (src, dst) in enumerate(pairs)]


def forward_kernel(
    lists_any, own_ref, other_ref, values_ref, out_ref, lists_ref, gathered, acc, sems
):
    lists_copy = pltpu.make_async_copy(lists_any, lists_ref, sems.at[0])
    lists_copy.start()
    total = values_ref.shape[0]
    gathered[0:HALF] = own_ref[...]
    gathered[HALF : 2 * HALF] = other_ref[...]
    acc[...] = jnp.zeros_like(acc)
    lists_copy.wait()

    def chunk(i, carry):
        for g in range(0, CHUNK, GROUP):
            slots = [i * CHUNK + g + k for k in range(GROUP)]
            products = [
                jnp.dot(values_ref[t], gathered[lists_ref[t]], preferred_element_type=f32)
                for t in slots
            ]
            for t, product in zip(slots, products):
                acc[lists_ref[2 * total + t]] += product
        return carry

    lax.fori_loop(0, values_ref.shape[0] // CHUNK, chunk, 0)
    out_ref[...] = acc[0:N_Y].astype(bf16)


def middle_kernel(
    scales_ref, parts_ref, scaled_ref, weight_ref, bias_ref, cotangent_ref, mixed_ref, send_ref
):
    total = jnp.sum(parts_ref[...].astype(f32), axis=0) + scaled_ref[0].astype(f32)
    aggregated = (scale_square(scales_ref) * total).astype(bf16)
    preact = (
        lax.dot_general(weight_ref[...], aggregated, (((1,), (1,)), ((), ())), preferred_element_type=f32)
        + bias_ref[...]
    )
    gate = jax.nn.sigmoid(preact)
    mixed_ref[...] = (preact * gate).astype(bf16)
    slope = gate * (1.0 + preact * (1.0 - gate))
    grad_pre = (cotangent_ref[...].astype(f32) * slope).astype(bf16)
    lifted = (scales_ref[...] * grad_pre.astype(f32)).astype(bf16)
    weight_part = jnp.dot(grad_pre, aggregated, preferred_element_type=f32).astype(bf16)
    send_ref[:, 0] = jnp.broadcast_to(lifted[None], (N_Y, F_OUT, BLOCK))
    send_ref[:, 1] = jnp.broadcast_to(weight_part[None], (N_Y, F_OUT, F_IN))


def backward_kernel(
    lists_any, group_ref, values_ref, mixed_ref, keep_ref, send_ref, mixed_any, lists_ref, acc, sems
):
    lists_copy = pltpu.make_async_copy(lists_any, lists_ref, sems.at[0])
    mixed_copy = pltpu.make_async_copy(mixed_ref, mixed_any, sems.at[1])
    lists_copy.start()
    mixed_copy.start()
    total = values_ref.shape[0]
    acc[...] = jnp.zeros_like(acc)
    lists_copy.wait()

    def chunk(i, carry):
        for g in range(0, CHUNK, GROUP):
            slots = [i * CHUNK + g + k for k in range(GROUP)]
            products = [
                jnp.dot(
                    group_ref[lists_ref[total + t], 0],
                    values_ref[t],
                    preferred_element_type=f32,
                )
                for t in slots
            ]
            for t, product in zip(slots, products):
                acc[lists_ref[3 * total + t]] += product
        return carry

    lax.fori_loop(0, values_ref.shape[0] // CHUNK, chunk, 0)
    weight_part = jnp.sum(group_ref[:, 1].astype(f32), axis=0).astype(bf16)
    for x in range(N_X):
        keep_ref[x, 0:N_Z] = acc[x * N_Z : (x + 1) * N_Z].astype(bf16)
        send_ref[x, 0:N_Z] = acc[HALF + x * N_Z : HALF + (x + 1) * N_Z].astype(bf16)
        keep_ref[x, N_Z] = weight_part
        send_ref[x, N_Z] = weight_part
    mixed_copy.wait()


def core_sum_kernel(keep_ref, recv_ref, out_ref):
    out_ref[...] = (keep_ref[...].astype(f32) + recv_ref[...].astype(f32)).astype(bf16)


def x_sum_kernel(recv_ref, out_ref):
    total = jnp.sum(recv_ref[...].astype(f32), axis=0).astype(bf16)
    out_ref[:, 0] = total[0:N_Z]
    out_ref[:, 1] = jnp.broadcast_to(total[N_Z][None], (N_Z, F_OUT, F_IN))


def final_kernel(scales_ref, recv_ref, sent_ref, weight_ref, grad_features_ref, grad_weight_ref):
    total = jnp.sum(recv_ref[...].astype(f32), axis=0)
    grad_scaled = scales_ref[...] * (total[0] + sent_ref[0, 0].astype(f32))
    turned = jnp.transpose(grad_scaled).astype(bf16)
    grad_features_ref[...] = jnp.dot(turned, weight_ref[...], preferred_element_type=f32).astype(bf16)
    node_total = BLOCK * N_Z * N_X * N_C * N_Y
    grad_weight_ref[...] = total[1] * (1.0 / np.sqrt(node_total))


def vmem():
    return pl.BlockSpec(memory_space=pltpu.VMEM)


def anywhere():
    return pl.BlockSpec(memory_space=pl.ANY)


def shards(
    features, degrees, tile_values, tile_row, tile_col, tile_count, weight, out_bias, cotangent
):
    slots = tile_values.shape[0]
    scales = lax.rsqrt(degrees.astype(f32) + 1.0).reshape(1, BLOCK)
    weight_t = weight.T
    cotangent_t = cotangent.T
    bias = jnp.broadcast_to(out_bias.astype(f32)[:, None], (F_OUT, BLOCK))
    slot_lists = [pltpu.SMEM((slots,), jnp.int32), pltpu.SMEM((slots,), jnp.int32), pltpu.SMEM((1,), jnp.int32)]
    params = pltpu.CompilerParams(vmem_limit_bytes=VMEM_BYTES)

    scaled = pl.pallas_call(
        start_kernel,
        out_shape=jax.ShapeDtypeStruct((N_Z, BLOCK, F_IN), bf16),
        in_specs=[vmem()] * 2,
        out_specs=vmem(),
        compiler_params=params,
        name="start",
    )(scales, features)
    by_z = exchange(scaled, 0)
    by_xz = exchange(jnp.broadcast_to(by_z[None], (N_X,) + by_z.shape), 1)
    own = by_xz.reshape(HALF, BLOCK, F_IN)
    other = swap_cores(own)
    lists = pl.pallas_call(
        lists_kernel,
        out_shape=jax.ShapeDtypeStruct((4 * slots,), jnp.int32),
        in_specs=[anywhere()] * 4,
        out_specs=pl.BlockSpec(memory_space=pltpu.SMEM),
        scratch_shapes=[*slot_lists, pltpu.SemaphoreType.DMA((3,))],
        compiler_params=params,
        name="lists",
    )(tile_row, tile_col, tile_count, own)

    parts = pl.pallas_call(
        forward_kernel,
        out_shape=jax.ShapeDtypeStruct((N_Y, BLOCK, F_IN), bf16),
        in_specs=[anywhere()] + [vmem()] * 3,
        out_specs=vmem(),
        scratch_shapes=[
            pltpu.SMEM((4 * slots,), jnp.int32),
            pltpu.VMEM((2 * HALF, BLOCK, F_IN), bf16),
            pltpu.VMEM((N_Y + 1, BLOCK, F_IN), f32),
            pltpu.SemaphoreType.DMA((1,)),
        ],
        compiler_params=params,
        name="forward",
    )(lists, own, other, tile_values)
    parts = exchange(parts, 3)

    mixed_here, send = pl.pallas_call(
        middle_kernel,
        out_shape=(
            jax.ShapeDtypeStruct((F_OUT, BLOCK), bf16),
            jax.ShapeDtypeStruct((N_Y, 2, F_OUT, BLOCK), bf16),
        ),
        in_specs=[vmem()] * 6,
        out_specs=(vmem(), vmem()),
        compiler_params=params,
        name="middle",
    )(scales, parts, scaled, weight_t, bias, cotangent_t)
    group = exchange(send, 3)

    half = jax.ShapeDtypeStruct((N_X, N_Z + 1, F_OUT, BLOCK), bf16)
    keep, away, mixed_t = pl.pallas_call(
        backward_kernel,
        out_shape=(half, half, jax.ShapeDtypeStruct((F_OUT, BLOCK), bf16)),
        in_specs=[anywhere()] + [vmem()] * 3,
        out_specs=(vmem(), vmem(), anywhere()),
        scratch_shapes=[
            pltpu.SMEM((4 * slots,), jnp.int32),
            pltpu.VMEM((2 * HALF + 1, F_OUT, BLOCK), f32),
            pltpu.SemaphoreType.DMA((2,)),
        ],
        compiler_params=params,
        name="backward",
    )(lists, group, tile_values, mixed_here)
    recv = swap_cores(away)
    by_core = pl.pallas_call(
        core_sum_kernel,
        out_shape=half,
        in_specs=[vmem()] * 2,
        out_specs=vmem(),
        compiler_params=params,
        name="core_sum",
    )(keep, recv)
    by_x = exchange(by_core, 1)
    by_x = pl.pallas_call(
        x_sum_kernel,
        out_shape=jax.ShapeDtypeStruct((N_Z, 2, F_OUT, BLOCK), bf16),
        in_specs=[vmem()],
        out_specs=vmem(),
        compiler_params=params,
        name="x_sum",
    )(by_x)
    last = exchange(by_x, 0)
    grad_features, grad_weight_t = pl.pallas_call(
        final_kernel,
        out_shape=(
            jax.ShapeDtypeStruct((BLOCK, F_IN), bf16),
            jax.ShapeDtypeStruct((F_OUT, F_IN), f32),
        ),
        in_specs=[vmem()] * 4,
        out_specs=(vmem(), vmem()),
        compiler_params=params,
        name="final",
    )(scales, last, send, weight_t)
    return (mixed_t.T, grad_features, grad_weight_t.T)


def solution(mesh):
    line = Mesh(np.asarray(mesh.devices).reshape(-1), ("d",))
    in_specs = (P("d", None), P("d"), P("d", None, None), P("d"), P("d"), P("d"), P(), P(), P("d", None))
    out_specs = (P("d", None), P("d", None), P())
    return jax.shard_map(shards, mesh=line, in_specs=in_specs, out_specs=out_specs, check_vma=False)
```

```python
import numpy as np

import jax
import jax.numpy as jnp
from jax import lax
from jax.experimental import pallas as pl
from jax.experimental.pallas import tpu as pltpu
from jax.sharding import Mesh, PartitionSpec as P

N_Z, N_X, N_C, N_Y = 8, 4, 2, 8
SIZES = (N_Z, N_X, N_C, N_Y)
BLOCK = 128
F_IN = 128
F_OUT = 64
CHUNK = 48
GROUP = 8
HALF = N_X * N_Z
VMEM_BYTES = 16 * 1024 * 1024
f32 = jnp.float32
bf16 = jnp.bfloat16


def scale_square(scales_ref):
    return jnp.transpose(jnp.broadcast_to(scales_ref[...], (BLOCK, BLOCK)))


def own_core():
    return jnp.bitwise_and(lax.shift_right_logical(lax.axis_index("d"), 3), 1)


def turned(number):
    low, high = jnp.bitwise_and(number, 1), lax.shift_right_logical(number, 2)
    return lax.shift_left(low, 2) + jnp.bitwise_and(number, 2) + high


def place_of(col, core):
    owner = lax.shift_right_logical(col, 3)
    z = lax.shift_right_logical(owner, 3)
    half = jnp.bitwise_and(owner, 1)
    x = jnp.bitwise_xor(jnp.bitwise_and(lax.shift_right_logical(owner, 1), 3), 2 * half)
    x = jnp.bitwise_xor(x, lax.shift_right_logical(x, 1))
    z = turned(jnp.bitwise_xor(jnp.bitwise_xor(z, half), N_Z - 1))
    return jnp.bitwise_xor(half, core) * HALF + x * N_Z + z


def place_in_group(row, core):
    return turned(jnp.bitwise_xor(jnp.bitwise_xor(jnp.bitwise_and(row, N_Y - 1), core), N_Y - 1))


def exchange(blocks, axis):
    size = SIZES[axis]
    numbers = np.moveaxis(np.arange(np.prod(SIZES)).reshape(SIZES), axis, -1)
    cores = numbers[..., 0].reshape(-1) // N_Y % N_C
    groups = []
    for group, core in zip(numbers.reshape(-1, size), cores):
        if size == 8:
            order = [k ^ 7 ^ int(core) for k in (0, 4, 2, 6, 1, 5, 3, 7)]
        else:
            order = [k ^ (2 * int(core)) for k in (0, 1, 3, 2)]
        groups.append([int(group[k]) for k in order])
    return lax.all_to_all(blocks, "d", 0, 0, axis_index_groups=groups)


def swap_cores(blocks):
    return lax.ppermute(blocks, "d", [(i, i ^ N_Y) for i in range(np.prod(SIZES))])


def start_kernel(scales_ref, features_ref, scaled_ref):
    scaled = (scale_square(scales_ref) * features_ref[...].astype(f32)).astype(bf16)
    scaled_ref[...] = jnp.broadcast_to(scaled[None], scaled_ref.shape)


def lists_kernel(rows_ref, cols_ref, count_ref, after_any, lists_ref):
    del after_any
    core = own_core()
    place = place_of(cols_ref[...], core)
    row = place_in_group(rows_ref[...], core)
    live = lax.broadcasted_iota(jnp.int32, row.shape, 1) < count_ref[0]
    lists_ref[0:1] = place
    lists_ref[1:2] = row
    lists_ref[2:3] = jnp.where(live, row, N_Y)
    lists_ref[3:4] = jnp.where(live, place, 2 * HALF)


def forward_kernel(
    lists_any, own_ref, other_ref, values_ref, out_ref, lists_ref, gathered, acc, sems
):
    lists_copy = pltpu.make_async_copy(lists_any, lists_ref, sems.at[0])
    lists_copy.start()
    gathered[0:HALF] = own_ref[...]
    gathered[HALF : 2 * HALF] = other_ref[...]
    acc[...] = jnp.zeros_like(acc)
    lists_copy.wait()

    def chunk(i, carry):
        for g in range(0, CHUNK, GROUP):
            slots = [i * CHUNK + g + k for k in range(GROUP)]
            products = [
                jnp.dot(values_ref[t], gathered[lists_ref[0, t]], preferred_element_type=f32)
                for t in slots
            ]
            for t, product in zip(slots, products):
                acc[lists_ref[2, t]] += product
        return carry

    lax.fori_loop(0, values_ref.shape[0] // CHUNK, chunk, 0)
    out_ref[...] = acc[0:N_Y].astype(bf16)


def middle_kernel(
    scales_ref, parts_ref, scaled_ref, weight_ref, bias_ref, cotangent_ref, mixed_ref, send_ref
):
    total = jnp.sum(parts_ref[...].astype(f32), axis=0) + scaled_ref[0].astype(f32)
    aggregated = (scale_square(scales_ref) * total).astype(bf16)
    preact = (
        lax.dot_general(weight_ref[...], aggregated, (((1,), (1,)), ((), ())), preferred_element_type=f32)
        + bias_ref[...]
    )
    gate = jax.nn.sigmoid(preact)
    mixed_ref[...] = (preact * gate).astype(bf16)
    slope = gate * (1.0 + preact * (1.0 - gate))
    grad_pre = (cotangent_ref[...].astype(f32) * slope).astype(bf16)
    lifted = (scales_ref[...] * grad_pre.astype(f32)).astype(bf16)
    weight_part = jnp.dot(grad_pre, aggregated, preferred_element_type=f32).astype(bf16)
    send_ref[:, 0] = jnp.broadcast_to(lifted[None], (N_Y, F_OUT, BLOCK))
    send_ref[:, 1] = jnp.broadcast_to(weight_part[None], (N_Y, F_OUT, F_IN))


def backward_kernel(
    lists_any, group_ref, values_ref, mixed_ref, keep_ref, send_ref, mixed_any, lists_ref, acc, sems
):
    lists_copy = pltpu.make_async_copy(lists_any, lists_ref, sems.at[0])
    mixed_copy = pltpu.make_async_copy(mixed_ref, mixed_any, sems.at[1])
    lists_copy.start()
    mixed_copy.start()
    acc[...] = jnp.zeros_like(acc)
    lists_copy.wait()

    def chunk(i, carry):
        for g in range(0, CHUNK, GROUP):
            slots = [i * CHUNK + g + k for k in range(GROUP)]
            products = [
                jnp.dot(
                    group_ref[lists_ref[1, t], 0],
                    values_ref[t],
                    preferred_element_type=f32,
                )
                for t in slots
            ]
            for t, product in zip(slots, products):
                acc[lists_ref[3, t]] += product
        return carry

    lax.fori_loop(0, values_ref.shape[0] // CHUNK, chunk, 0)
    weight_part = jnp.sum(group_ref[:, 1].astype(f32), axis=0).astype(bf16)
    for x in range(N_X):
        keep_ref[x, 0:N_Z] = acc[x * N_Z : (x + 1) * N_Z].astype(bf16)
        send_ref[x, 0:N_Z] = acc[HALF + x * N_Z : HALF + (x + 1) * N_Z].astype(bf16)
        keep_ref[x, N_Z] = weight_part
        send_ref[x, N_Z] = weight_part
    mixed_copy.wait()


def core_sum_kernel(keep_ref, recv_ref, out_ref):
    out_ref[...] = (keep_ref[...].astype(f32) + recv_ref[...].astype(f32)).astype(bf16)


def x_sum_kernel(recv_ref, out_ref):
    total = jnp.sum(recv_ref[...].astype(f32), axis=0).astype(bf16)
    out_ref[:, 0] = total[0:N_Z]
    out_ref[:, 1] = jnp.broadcast_to(total[N_Z][None], (N_Z, F_OUT, F_IN))


def final_kernel(scales_ref, recv_ref, sent_ref, weight_ref, grad_features_ref, grad_weight_ref):
    total = jnp.sum(recv_ref[...].astype(f32), axis=0)
    grad_scaled = scales_ref[...] * (total[0] + sent_ref[0, 0].astype(f32))
    turned = jnp.transpose(grad_scaled).astype(bf16)
    grad_features_ref[...] = jnp.dot(turned, weight_ref[...], preferred_element_type=f32).astype(bf16)
    node_total = BLOCK * N_Z * N_X * N_C * N_Y
    grad_weight_ref[...] = total[1] * (1.0 / np.sqrt(node_total))


def vmem():
    return pl.BlockSpec(memory_space=pltpu.VMEM)


def anywhere():
    return pl.BlockSpec(memory_space=pl.ANY)


def shards(
    features, degrees, tile_values, tile_row, tile_col, tile_count, weight, out_bias, cotangent
):
    slots = tile_values.shape[0]
    scales = lax.rsqrt(degrees.astype(f32) + 1.0).reshape(1, BLOCK)
    weight_t = weight.T
    cotangent_t = cotangent.T
    bias = jnp.broadcast_to(out_bias.astype(f32)[:, None], (F_OUT, BLOCK))
    params = pltpu.CompilerParams(vmem_limit_bytes=VMEM_BYTES)

    scaled = pl.pallas_call(
        start_kernel,
        out_shape=jax.ShapeDtypeStruct((N_Z, BLOCK, F_IN), bf16),
        in_specs=[vmem()] * 2,
        out_specs=vmem(),
        compiler_params=params,
        name="start",
    )(scales, features)
    by_z = exchange(scaled, 0)
    by_xz = exchange(jnp.broadcast_to(by_z[None], (N_X,) + by_z.shape), 1)
    own = by_xz.reshape(HALF, BLOCK, F_IN)
    other = swap_cores(own)
    lists = pl.pallas_call(
        lists_kernel,
        out_shape=jax.ShapeDtypeStruct((4, slots), jnp.int32),
        in_specs=[vmem(), vmem(), pl.BlockSpec(memory_space=pltpu.SMEM), anywhere()],
        out_specs=vmem(),
        compiler_params=params,
        name="lists",
    )(tile_row.reshape(1, slots), tile_col.reshape(1, slots), tile_count, own)

    parts = pl.pallas_call(
        forward_kernel,
        out_shape=jax.ShapeDtypeStruct((N_Y, BLOCK, F_IN), bf16),
        in_specs=[anywhere()] + [vmem()] * 3,
        out_specs=vmem(),
        scratch_shapes=[
            pltpu.SMEM((4, slots), jnp.int32),
            pltpu.VMEM((2 * HALF, BLOCK, F_IN), bf16),
            pltpu.VMEM((N_Y + 1, BLOCK, F_IN), f32),
            pltpu.SemaphoreType.DMA((1,)),
        ],
        compiler_params=params,
        name="forward",
    )(lists, own, other, tile_values)
    parts = exchange(parts, 3)

    mixed_here, send = pl.pallas_call(
        middle_kernel,
        out_shape=(
            jax.ShapeDtypeStruct((F_OUT, BLOCK), bf16),
            jax.ShapeDtypeStruct((N_Y, 2, F_OUT, BLOCK), bf16),
        ),
        in_specs=[vmem()] * 6,
        out_specs=(vmem(), vmem()),
        compiler_params=params,
        name="middle",
    )(scales, parts, scaled, weight_t, bias, cotangent_t)
    group = exchange(send, 3)

    half = jax.ShapeDtypeStruct((N_X, N_Z + 1, F_OUT, BLOCK), bf16)
    keep, away, mixed_t = pl.pallas_call(
        backward_kernel,
        out_shape=(half, half, jax.ShapeDtypeStruct((F_OUT, BLOCK), bf16)),
        in_specs=[anywhere()] + [vmem()] * 3,
        out_specs=(vmem(), vmem(), anywhere()),
        scratch_shapes=[
            pltpu.SMEM((4, slots), jnp.int32),
            pltpu.VMEM((2 * HALF + 1, F_OUT, BLOCK), f32),
            pltpu.SemaphoreType.DMA((2,)),
        ],
        compiler_params=params,
        name="backward",
    )(lists, group, tile_values, mixed_here)
    recv = swap_cores(away)
    by_core = pl.pallas_call(
        core_sum_kernel,
        out_shape=half,
        in_specs=[vmem()] * 2,
        out_specs=vmem(),
        compiler_params=params,
        name="core_sum",
    )(keep, recv)
    by_x = exchange(by_core, 1)
    by_x = pl.pallas_call(
        x_sum_kernel,
        out_shape=jax.ShapeDtypeStruct((N_Z, 2, F_OUT, BLOCK), bf16),
        in_specs=[vmem()],
        out_specs=vmem(),
        compiler_params=params,
        name="x_sum",
    )(by_x)
    last = exchange(by_x, 0)
    grad_features, grad_weight_t = pl.pallas_call(
        final_kernel,
        out_shape=(
            jax.ShapeDtypeStruct((BLOCK, F_IN), bf16),
            jax.ShapeDtypeStruct((F_OUT, F_IN), f32),
        ),
        in_specs=[vmem()] * 4,
        out_specs=(vmem(), vmem()),
        compiler_params=params,
        name="final",
    )(scales, last, send, weight_t)
    return (mixed_t.T, grad_features, grad_weight_t.T)


def solution(mesh):
    line = Mesh(np.asarray(mesh.devices).reshape(-1), ("d",))
    in_specs = (P("d", None), P("d"), P("d", None, None), P("d"), P("d"), P("d"), P(), P(), P("d", None))
    out_specs = (P("d", None), P("d", None), P())
    return jax.shard_map(shards, mesh=line, in_specs=in_specs, out_specs=out_specs, check_vma=False)
```

```python
import numpy as np

import jax
import jax.numpy as jnp
from jax import lax
from jax.experimental import pallas as pl
from jax.experimental.pallas import tpu as pltpu
from jax.sharding import Mesh, PartitionSpec as P

N_Z, N_X, N_C, N_Y = 8, 4, 2, 8
SIZES = (N_Z, N_X, N_C, N_Y)
BLOCK = 128
F_IN = 128
F_OUT = 64
CHUNK = 96
GROUP = 8
HALF = N_X * N_Z
VMEM_BYTES = 16 * 1024 * 1024
f32 = jnp.float32
bf16 = jnp.bfloat16


def scale_square(scales_ref):
    return jnp.transpose(jnp.broadcast_to(scales_ref[...], (BLOCK, BLOCK)))


def own_core():
    return jnp.bitwise_and(lax.shift_right_logical(lax.axis_index("d"), 3), 1)


def turned(number):
    low, high = jnp.bitwise_and(number, 1), lax.shift_right_logical(number, 2)
    return lax.shift_left(low, 2) + jnp.bitwise_and(number, 2) + high


def place_of(col, core):
    owner = lax.shift_right_logical(col, 3)
    z = lax.shift_right_logical(owner, 3)
    half = jnp.bitwise_and(owner, 1)
    x = jnp.bitwise_xor(jnp.bitwise_and(lax.shift_right_logical(owner, 1), 3), 2 * half)
    x = jnp.bitwise_xor(x, lax.shift_right_logical(x, 1))
    z = turned(jnp.bitwise_xor(jnp.bitwise_xor(z, half), N_Z - 1))
    return jnp.bitwise_xor(half, core) * HALF + x * N_Z + z


def place_in_group(row, core):
    return turned(jnp.bitwise_xor(jnp.bitwise_xor(jnp.bitwise_and(row, N_Y - 1), core), N_Y - 1))


def exchange(blocks, axis):
    size = SIZES[axis]
    numbers = np.moveaxis(np.arange(np.prod(SIZES)).reshape(SIZES), axis, -1)
    cores = numbers[..., 0].reshape(-1) // N_Y % N_C
    groups = []
    for group, core in zip(numbers.reshape(-1, size), cores):
        if size == 8:
            order = [k ^ 7 ^ int(core) for k in (0, 4, 2, 6, 1, 5, 3, 7)]
        else:
            order = [k ^ (2 * int(core)) for k in (0, 1, 3, 2)]
        groups.append([int(group[k]) for k in order])
    return lax.all_to_all(blocks, "d", 0, 0, axis_index_groups=groups)


def swap_cores(blocks):
    return lax.ppermute(blocks, "d", [(i, i ^ N_Y) for i in range(np.prod(SIZES))])


def start_kernel(scales_ref, features_ref, scaled_ref):
    scaled = (scale_square(scales_ref) * features_ref[...].astype(f32)).astype(bf16)
    scaled_ref[...] = jnp.broadcast_to(scaled[None], scaled_ref.shape)


def lists_kernel(rows_ref, cols_ref, count_ref, after_any, lists_ref):
    del after_any
    core = own_core()
    place = place_of(cols_ref[...], core)
    row = place_in_group(rows_ref[...], core)
    live = lax.broadcasted_iota(jnp.int32, row.shape, 1) < count_ref[0]
    lists_ref[0:1] = place
    lists_ref[1:2] = row
    lists_ref[2:3] = jnp.where(live, row, N_Y)
    lists_ref[3:4] = jnp.where(live, place, 2 * HALF)


def forward_kernel(
    lists_any, own_ref, other_ref, values_ref, out_ref, lists_ref, gathered, acc, sems
):
    lists_copy = pltpu.make_async_copy(lists_any, lists_ref, sems.at[0])
    lists_copy.start()
    gathered[0:HALF] = own_ref[...]
    gathered[HALF : 2 * HALF] = other_ref[...]
    acc[...] = jnp.zeros_like(acc)
    lists_copy.wait()

    def chunk(i, carry):
        for g in range(0, CHUNK, GROUP):
            slots = [i * CHUNK + g + k for k in range(GROUP)]
            products = [
                jnp.dot(values_ref[t], gathered[lists_ref[0, t]], preferred_element_type=f32)
                for t in slots
            ]
            for t, product in zip(slots, products):
                acc[lists_ref[2, t]] += product
        return carry

    lax.fori_loop(0, values_ref.shape[0] // CHUNK, chunk, 0)
    out_ref[...] = acc[0:N_Y].astype(bf16)


def middle_kernel(
    scales_ref, parts_ref, scaled_ref, weight_ref, bias_ref, cotangent_ref, mixed_ref, send_ref
):
    total = jnp.sum(parts_ref[...].astype(f32), axis=0) + scaled_ref[0].astype(f32)
    aggregated = (scale_square(scales_ref) * total).astype(bf16)
    preact = (
        lax.dot_general(weight_ref[...], aggregated, (((1,), (1,)), ((), ())), preferred_element_type=f32)
        + bias_ref[...]
    )
    gate = jax.nn.sigmoid(preact)
    mixed_ref[...] = (preact * gate).astype(bf16)
    slope = gate * (1.0 + preact * (1.0 - gate))
    grad_pre = (cotangent_ref[...].astype(f32) * slope).astype(bf16)
    lifted = (scales_ref[...] * grad_pre.astype(f32)).astype(bf16)
    weight_part = jnp.dot(grad_pre, aggregated, preferred_element_type=f32).astype(bf16)
    send_ref[:, 0] = jnp.broadcast_to(lifted[None], (N_Y, F_OUT, BLOCK))
    send_ref[:, 1] = jnp.broadcast_to(weight_part[None], (N_Y, F_OUT, F_IN))


def backward_kernel(
    lists_any, group_ref, values_ref, mixed_ref, keep_ref, send_ref, mixed_any, lists_ref, acc, sems
):
    lists_copy = pltpu.make_async_copy(lists_any, lists_ref, sems.at[0])
    mixed_copy = pltpu.make_async_copy(mixed_ref, mixed_any, sems.at[1])
    lists_copy.start()
    mixed_copy.start()
    acc[...] = jnp.zeros_like(acc)
    lists_copy.wait()

    def chunk(i, carry):
        for g in range(0, CHUNK, GROUP):
            slots = [i * CHUNK + g + k for k in range(GROUP)]
            products = [
                jnp.dot(
                    group_ref[lists_ref[1, t], 0],
                    values_ref[t],
                    preferred_element_type=f32,
                )
                for t in slots
            ]
            for t, product in zip(slots, products):
                acc[lists_ref[3, t]] += product
        return carry

    lax.fori_loop(0, values_ref.shape[0] // CHUNK, chunk, 0)
    weight_part = jnp.sum(group_ref[:, 1].astype(f32), axis=0).astype(bf16)
    for x in range(N_X):
        keep_ref[x, 0:N_Z] = acc[x * N_Z : (x + 1) * N_Z].astype(bf16)
        send_ref[x, 0:N_Z] = acc[HALF + x * N_Z : HALF + (x + 1) * N_Z].astype(bf16)
        keep_ref[x, N_Z] = weight_part
        send_ref[x, N_Z] = weight_part
    mixed_copy.wait()


def core_sum_kernel(keep_ref, recv_ref, out_ref):
    out_ref[...] = (keep_ref[...].astype(f32) + recv_ref[...].astype(f32)).astype(bf16)


def x_sum_kernel(recv_ref, out_ref):
    total = jnp.sum(recv_ref[...].astype(f32), axis=0).astype(bf16)
    out_ref[:, 0] = total[0:N_Z]
    out_ref[:, 1] = jnp.broadcast_to(total[N_Z][None], (N_Z, F_OUT, F_IN))


def final_kernel(scales_ref, recv_ref, sent_ref, weight_ref, grad_features_ref, grad_weight_ref):
    total = jnp.sum(recv_ref[...].astype(f32), axis=0)
    grad_scaled = scales_ref[...] * (total[0] + sent_ref[0, 0].astype(f32))
    turned = jnp.transpose(grad_scaled).astype(bf16)
    grad_features_ref[...] = jnp.dot(turned, weight_ref[...], preferred_element_type=f32).astype(bf16)
    node_total = BLOCK * N_Z * N_X * N_C * N_Y
    grad_weight_ref[...] = total[1] * (1.0 / np.sqrt(node_total))


def vmem():
    return pl.BlockSpec(memory_space=pltpu.VMEM)


def anywhere():
    return pl.BlockSpec(memory_space=pl.ANY)


def shards(
    features, degrees, tile_values, tile_row, tile_col, tile_count, weight, out_bias, cotangent
):
    slots = tile_values.shape[0]
    scales = lax.rsqrt(degrees.astype(f32) + 1.0).reshape(1, BLOCK)
    weight_t = weight.T
    cotangent_t = cotangent.T
    bias = jnp.broadcast_to(out_bias.astype(f32)[:, None], (F_OUT, BLOCK))
    params = pltpu.CompilerParams(vmem_limit_bytes=VMEM_BYTES)

    scaled = pl.pallas_call(
        start_kernel,
        out_shape=jax.ShapeDtypeStruct((N_Z, BLOCK, F_IN), bf16),
        in_specs=[vmem()] * 2,
        out_specs=vmem(),
        compiler_params=params,
        name="start",
    )(scales, features)
    by_z = exchange(scaled, 0)
    by_xz = exchange(jnp.broadcast_to(by_z[None], (N_X,) + by_z.shape), 1)
    own = by_xz.reshape(HALF, BLOCK, F_IN)
    other = swap_cores(own)
    lists = pl.pallas_call(
        lists_kernel,
        out_shape=jax.ShapeDtypeStruct((4, slots), jnp.int32),
        in_specs=[vmem(), vmem(), pl.BlockSpec(memory_space=pltpu.SMEM), anywhere()],
        out_specs=vmem(),
        compiler_params=params,
        name="lists",
    )(tile_row.reshape(1, slots), tile_col.reshape(1, slots), tile_count, own)

    parts = pl.pallas_call(
        forward_kernel,
        out_shape=jax.ShapeDtypeStruct((N_Y, BLOCK, F_IN), bf16),
        in_specs=[anywhere()] + [vmem()] * 3,
        out_specs=vmem(),
        scratch_shapes=[
            pltpu.SMEM((4, slots), jnp.int32),
            pltpu.VMEM((2 * HALF, BLOCK, F_IN), bf16),
            pltpu.VMEM((N_Y + 1, BLOCK, F_IN), f32),
            pltpu.SemaphoreType.DMA((1,)),
        ],
        compiler_params=params,
        name="forward",
    )(lists, own, other, tile_values)
    parts = exchange(parts, 3)

    mixed_here, send = pl.pallas_call(
        middle_kernel,
        out_shape=(
            jax.ShapeDtypeStruct((F_OUT, BLOCK), bf16),
            jax.ShapeDtypeStruct((N_Y, 2, F_OUT, BLOCK), bf16),
        ),
        in_specs=[vmem()] * 6,
        out_specs=(vmem(), vmem()),
        compiler_params=params,
        name="middle",
    )(scales, parts, scaled, weight_t, bias, cotangent_t)
    group = exchange(send, 3)

    half = jax.ShapeDtypeStruct((N_X, N_Z + 1, F_OUT, BLOCK), bf16)
    keep, away, mixed_t = pl.pallas_call(
        backward_kernel,
        out_shape=(half, half, jax.ShapeDtypeStruct((F_OUT, BLOCK), bf16)),
        in_specs=[anywhere()] + [vmem()] * 3,
        out_specs=(vmem(), vmem(), anywhere()),
        scratch_shapes=[
            pltpu.SMEM((4, slots), jnp.int32),
            pltpu.VMEM((2 * HALF + 1, F_OUT, BLOCK), f32),
            pltpu.SemaphoreType.DMA((2,)),
        ],
        compiler_params=params,
        name="backward",
    )(lists, group, tile_values, mixed_here)
    recv = swap_cores(away)
    by_core = pl.pallas_call(
        core_sum_kernel,
        out_shape=half,
        in_specs=[vmem()] * 2,
        out_specs=vmem(),
        compiler_params=params,
        name="core_sum",
    )(keep, recv)
    by_x = exchange(by_core, 1)
    by_x = pl.pallas_call(
        x_sum_kernel,
        out_shape=jax.ShapeDtypeStruct((N_Z, 2, F_OUT, BLOCK), bf16),
        in_specs=[vmem()],
        out_specs=vmem(),
        compiler_params=params,
        name="x_sum",
    )(by_x)
    last = exchange(by_x, 0)
    grad_features, grad_weight_t = pl.pallas_call(
        final_kernel,
        out_shape=(
            jax.ShapeDtypeStruct((BLOCK, F_IN), bf16),
            jax.ShapeDtypeStruct((F_OUT, F_IN), f32),
        ),
        in_specs=[vmem()] * 4,
        out_specs=(vmem(), vmem()),
        compiler_params=params,
        name="final",
    )(scales, last, send, weight_t)
    return (mixed_t.T, grad_features, grad_weight_t.T)


def solution(mesh):
    line = Mesh(np.asarray(mesh.devices).reshape(-1), ("d",))
    in_specs = (P("d", None), P("d"), P("d", None, None), P("d"), P("d"), P("d"), P(), P(), P("d", None))
    out_specs = (P("d", None), P("d", None), P())
    return jax.shard_map(shards, mesh=line, in_specs=in_specs, out_specs=out_specs, check_vma=False)
```
